512 devices in a mesh: seq: 64 (over z, y), head: 8 (over x, core).
Axes of the slice: x: 4, y: 4, z: 16, core: 2. Of those that a mesh axis runs over, the one named last changes fastest.
Arguments:
- queries: bfloat16 [16384, 8192], P(('seq', 'head')), may hold values from -6 to 6
- keys: bfloat16 [16384, 8192], P(('seq', 'head')), may hold values from -6 to 6
- values: bfloat16 [16384, 8192], P(('seq', 'head')), may hold values from -6 to 6
- landmarks: bfloat16 [256, 8192], P('seq', 'head'), may hold values from -6 to 6
- grad_out: bfloat16 [16384, 8192], P(('seq', 'head')), may hold values from -6 to 6
- selections: int32 [256, 16], P('seq'), may hold values from -1 to 255, as said below
Outputs:
- attended: bfloat16 [16384, 8192], P('seq', 'head')
- grad_queries: bfloat16 [16384, 8192], P('seq', 'head')
- grad_keys: bfloat16 [16384, 8192], P('seq', 'head')
- grad_values: bfloat16 [16384, 8192], P('seq', 'head')
- grad_landmarks: bfloat16 [256, 8192], P('seq', 'head')
The draws below stay inside these ranges and needn't reach their ends.
Inputs may be any that keep to these rules, and one draw needn't show every extreme that they name: `selections`: entry 0 of query block b's list is b. The other live entries are distinct blocks b - o with 1 <= o <= 16; live entries come first and -1 fills the rest. The list of the last block is full.
All inputs are finite; a program needn't handle non-finite values.
Results may differ from the reference program's by a relative error of at most 0.017.
Values may be sent and summed in bfloat16 or wider, within the bound.
A program may use at most 128 MiB of HBM per device.

```python
from functools import partial
import jax
import jax.numpy as jnp
from jax import lax

HEADS = 64
HD = 128
BLOCK = 64
SEL = 16
REACH = 4
TOK_DEV = 256
TOKENS = 16384
NBLK = 256
WIDTH = 8192


strengths = (3.0, 4.25, 5.5)


peak_high = 5.5


peak_next = 5.46875


def make_selections(key):
    key_rank, key_count = jax.random.split(key)
    window = REACH * (TOK_DEV // BLOCK)
    blocks = jnp.arange(NBLK, dtype=jnp.int32)[:, None]
    offsets = jnp.broadcast_to(jnp.arange(1, window + 1, dtype=jnp.int32)[None, :], (NBLK, window))
    usable = blocks - offsets >= 0
    jitter = jax.random.randint(key_rank, (NBLK, window), 0, 1 << 20)
    ranking = jnp.where(usable, 0, 1 << 28) + jitter * window + jnp.arange(window, dtype=jnp.int32)[None, :]
    ranked = jnp.argsort(ranking, axis=1)[:, :SEL - 1]
    picked = jnp.take_along_axis(offsets, ranked, axis=1)
    picked_usable = jnp.take_along_axis(usable, ranked, axis=1)
    counts = jax.random.randint(key_count, (NBLK, 1), SEL // 4, SEL + 1)
    counts = jnp.where(blocks == NBLK - 1, SEL, counts)
    slot_pos = jnp.arange(1, SEL, dtype=jnp.int32)[None, :]
    chosen = picked_usable & (slot_pos < counts)
    others = jnp.where(chosen, blocks - picked, -1)
    return jnp.concatenate([blocks, others], axis=1).astype(jnp.int32)


def draw_selections(key, part):
    key = jax.random.fold_in(key, 7)
    return make_selections(key)


def planted(key):
    chosen = make_selections(jax.random.fold_in(key, 7))
    key_pattern, key_head = jax.random.split(jax.random.fold_in(key, 11), 2)
    pattern = jnp.where(jax.random.bernoulli(key_pattern, 0.5, (HD,)), 1.0, -1.0).astype(jnp.float32)
    stride = NBLK // 3
    aligned = (NBLK - 1 - stride * jnp.arange(3, dtype=jnp.int32)).astype(jnp.int32)
    second = chosen[aligned, 1].astype(jnp.int32)
    first_head = jax.random.randint(key_head, (), 0, HEADS)
    head_ids = ((first_head + HEADS // 3 * jnp.arange(3, dtype=jnp.int32)) % HEADS).astype(jnp.int32)
    return (pattern, aligned, second, head_ids)


def base_field(key, row_count, spread):
    key_jitter, key_scale = jax.random.split(key)
    jitter = jax.random.normal(key_jitter, (row_count, WIDTH), jnp.float32)
    scales = jnp.exp(jax.random.uniform(key_scale, (row_count, 1), jnp.float32, -spread, spread))
    return jnp.clip(jitter * scales, -6.0, 6.0)


def implant(target, row_id, head_id, vector):
    corner = (jnp.asarray(row_id).astype(jnp.int32), (head_id * HD).astype(jnp.int32))
    return lax.dynamic_update_slice(target, vector[None, :], corner)


def draw_queries(key, part):
    pattern, aligned, second, head_ids = planted(key)
    key = jax.random.fold_in(key, 21)
    spread = 0.0
    result = base_field(key, TOKENS, spread)
    for number in range(3):
        result = implant(result, aligned[number] * BLOCK + BLOCK - 1, head_ids[number], strengths[number] * pattern)
    return result.astype(jnp.bfloat16)


def draw_keys(key, part):
    pattern, aligned, second, head_ids = planted(key)
    key = jax.random.fold_in(key, 22)
    spread = 0.0
    result = base_field(key, TOKENS, spread)
    for number in range(3):
        result = implant(result, aligned[number] * BLOCK + BLOCK - 1, head_ids[number], peak_high * pattern)
        result = implant(result, aligned[number] * BLOCK + BLOCK - 2, head_ids[number], peak_next * pattern)
    return result.astype(jnp.bfloat16)


def draw_landmarks(key, part):
    pattern, aligned, second, head_ids = planted(key)
    key = jax.random.fold_in(key, 23)
    spread = 0.0
    result = base_field(key, NBLK, spread)
    for number in range(3):
        result = implant(result, aligned[number], head_ids[number], peak_high * pattern)
        result = implant(result, second[number], head_ids[number], peak_next * pattern)
    return result.astype(jnp.bfloat16)


def steps_of(rng, dims, cuts, smallest, top_value):
    factor_of = 1.0
    for dim, shards_of in cuts:
        heights = jax.random.uniform(jax.random.fold_in(jax.random.fold_in(rng, 6), dim), (shards_of,), jnp.float32, smallest / len(cuts), top_value / len(cuts))
        factor_of = factor_of * jnp.repeat(jnp.exp(heights), dims[dim] // shards_of).reshape((-1,) + (1,) * (len(dims) - 1 - dim))
    return factor_of


def gaussian(rng, extent, scale, limit, cuts=(), kind=jnp.bfloat16):
    values = scale * jax.random.normal(rng, extent, jnp.float32)
    if cuts:
        values = values * steps_of(rng, extent, cuts, -0.22, 0.18)
    return jnp.clip(values, -limit, limit).astype(kind)


def setup_inputs(seed: int = 0) -> dict:
    key_of = jax.random.split(jax.random.key(seed), 7)
    queries = draw_queries(jax.random.fold_in(key_of[6], 71), 0)
    keys = draw_keys(jax.random.fold_in(key_of[6], 71), 0)
    values = gaussian(key_of[2], (TOKENS, WIDTH), 1.0, 6.0, ((0, 512),))
    landmarks = draw_landmarks(jax.random.fold_in(key_of[6], 71), 0)
    grad_out = gaussian(key_of[4], (TOKENS, WIDTH), 1.0, 6.0, ((0, 512),))
    selections = draw_selections(jax.random.fold_in(key_of[6], 71), 0)
    return dict(queries=queries, keys=keys, values=values, landmarks=landmarks, grad_out=grad_out, selections=selections)


def attend_block(query_blk, key_win, value_win, mark_win, slot_index, slot_live, own_slot, head_count):
    block_len = query_blk.shape[0]
    head_dim = query_blk.shape[1] // head_count
    pick_count = slot_index.shape[0]
    scale_q = head_dim ** (-0.5)
    query_heads = query_blk.astype(jnp.bfloat16).reshape(block_len, head_count, head_dim)
    key_sel = jnp.take(key_win, slot_index, axis=0).astype(jnp.bfloat16).reshape(pick_count, block_len, head_count, head_dim)
    value_sel = jnp.take(value_win, slot_index, axis=0).astype(jnp.bfloat16).reshape(pick_count, block_len, head_count, head_dim)
    mark_sel = jnp.take(mark_win, slot_index, axis=0).astype(jnp.bfloat16).reshape(pick_count, head_count, head_dim)
    scores = jnp.einsum('ihd,ejhd->heij', query_heads, key_sel, preferred_element_type=jnp.float32) * scale_q
    row_pos = jnp.arange(block_len)[:, None]
    col_pos = jnp.arange(block_len)[None, :]
    masked = (slot_index == own_slot)[:, None, None] & (col_pos > row_pos)[None, :, :]
    scores = jnp.where(masked[None], -1e+30, scores)
    inner_w = jax.nn.softmax(scores, axis=-1)
    coarse = jnp.einsum('ihd,ehd->hie', query_heads, mark_sel, preferred_element_type=jnp.float32) * scale_q
    coarse = jnp.where(slot_live[None, None, :], coarse, -1e+30)
    gate_w = jax.nn.softmax(coarse, axis=-1)
    weights = (inner_w * jnp.transpose(gate_w, (0, 2, 1))[:, :, :, None]).astype(jnp.bfloat16)
    result = jnp.einsum('heij,ejhd->ihd', weights, value_sel, preferred_element_type=jnp.float32)
    return result.reshape(block_len, head_count * head_dim)

def forward(query_f, key_f, value_f, mark_f, selections):
    blocks_all = selections.shape[0]
    features = query_f.shape[1]
    block_len = query_f.shape[0] // blocks_all
    key_win = key_f.reshape(blocks_all, block_len, features)
    value_win = value_f.reshape(blocks_all, block_len, features)
    query_blocks = query_f.reshape(blocks_all, block_len, features)
    own_ids = jnp.arange(blocks_all, dtype=jnp.int32)
    slot_live = selections >= 0
    slot_index = jnp.where(slot_live, selections, own_ids[:, None]).astype(jnp.int32)
    step_fn = jax.checkpoint(partial(attend_block, head_count=HEADS))

    def per_block(pieces):
        return step_fn(pieces[0], key_win, value_win, mark_f, pieces[1], pieces[2], pieces[3])
    result = lax.map(per_block, (query_blocks, slot_index, slot_live, own_ids))
    return result.reshape(-1, features)

def reference(queries, keys, values, landmarks, grad_out, selections):
    attended, pull = jax.vjp(partial(forward, selections=selections), queries.astype(jnp.float32), keys.astype(jnp.float32), values.astype(jnp.float32), landmarks.astype(jnp.float32))
    grads = pull(grad_out.astype(jnp.float32))
    return (attended.astype(jnp.bfloat16), grads[0].astype(jnp.bfloat16), grads[1].astype(jnp.bfloat16), grads[2].astype(jnp.bfloat16), grads[3].astype(jnp.bfloat16))
```

```python
import jax
import jax.numpy as jnp
from jax import lax
from jax.experimental import pallas as pl
from jax.experimental.pallas import tpu as pltpu
from jax.sharding import PartitionSpec as P

HD = 128
BLOCK = 64
HPD = 2
CH = 256
CB = CH // BLOCK
SCALE = HD ** (-0.5)
LOG2E = 1.4426950408889634
NT = (((1,), (1,)), ((), ()))
NN = (((1,), (0,)), ((), ()))
TN = (((0,), (0,)), ((), ()))


def dot(a, b, dims):
    return lax.dot_general(a, b, dims, preferred_element_type=jnp.float32)


def rows(c):
    return pl.ds(pl.multiple_of(c * CH, CH), CH)


def lanes(h):
    return slice(h * HD, (h + 1) * HD)


def gate_tile(t, first, q, marks, sel, gates):
    row = lax.broadcasted_iota(jnp.int32, (64, CH), 0)
    sub = row % 8
    block = first + (row // 8) * CB + sub
    block = jnp.where((sub < CB) & (block >= 0), block, -2)
    picks = sel[t]
    live = block == picks[0:1]
    for e in range(1, picks.shape[0]):
        live = live | (block == picks[e:e + 1])
    for h in range(HPD):
        mk = marks[:, :, lanes(h)].reshape(64, HD).astype(jnp.bfloat16)
        coarse = dot(mk, q[rows(t), lanes(h)], NT) * SCALE
        coarse = jnp.where(live, coarse, -1e30)
        top = jnp.max(coarse, axis=0, keepdims=True)
        ex = jnp.exp(coarse - top)
        gates[h, t] = (ex / jnp.sum(ex, axis=0, keepdims=True)).reshape(8, 8, CH)


def cell(t, kc, diag, q, d, k, v, kt, vt, gates, dgates, ot, dqt, dk, dv):
    for h in range(HPD):
        qh = q[rows(t), lanes(h)]
        dh = d[rows(t), lanes(h)]
        s = dot(k[rows(kc), lanes(h)], qh, NT)
        g = dot(v[rows(kc), lanes(h)], dh, NT)
        if diag:
            j = lax.broadcasted_iota(jnp.int32, (CH, CH), 0)
            i = lax.broadcasted_iota(jnp.int32, (CH, CH), 1)
            s = jnp.where(j > i, -1e30, s)
        s = s.reshape(CB, BLOCK, CH)
        g = g.reshape(CB, BLOCK, CH)
        top = jnp.max(s, axis=1, keepdims=True)
        p = jnp.exp2((s - top) * (SCALE * LOG2E))
        rz = 1.0 / jnp.sum(p, axis=1, keepdims=True)
        dg = jnp.sum(p * g, axis=1, keepdims=True) * rz
        gate = gates[h, t, kc][0:CB].reshape(CB, 1, CH)
        w = p * (gate * rz)
        ds = w * (g - dg)
        dgates[h, t, kc, 0:CB] = dg.reshape(CB, CH)
        wb = w.astype(jnp.bfloat16).reshape(CH, CH)
        sb = ds.astype(jnp.bfloat16).reshape(CH, CH)
        ot[h, t] += dot(vt[h, kc], wb, NN)
        dqt[h, t] += dot(kt[h, kc], sb, NN)
        dv[kc, :, lanes(h)] += dot(wb, dh, NN)
        dk[kc, :, lanes(h)] += dot(sb, qh, NN)


def transpose_chunk(kc, src, dst):
    for h in range(HPD):
        dst[h, kc] = src[rows(kc), lanes(h)].T


def close_tile(t, q, marks, gates, dgates, ot, dqt, dm, o_out, dq_out):
    for h in range(HPD):
        gate = gates[h, t].reshape(64, CH)
        dg = dgates[h, t].reshape(64, CH)
        dc = gate * (dg - jnp.sum(gate * dg, axis=0, keepdims=True))
        dcb = dc.astype(jnp.bfloat16)
        mk = marks[:, :, lanes(h)].reshape(64, HD).astype(jnp.bfloat16)
        dq = dqt[h, t] + dot(mk, dcb, TN)
        o_out[rows(t), lanes(h)] = ot[h, t].T.astype(jnp.bfloat16)
        dq_out[rows(t), lanes(h)] = (dq * SCALE).T.astype(jnp.bfloat16)
        dm[:, :, lanes(h)] += (dot(dcb, q[rows(t), lanes(h)], NN) * SCALE).reshape(8, 8, HD)


def all_scratch():
    f = jnp.float32
    return [
        pltpu.VMEM((HPD, 8, HD, CH), jnp.bfloat16),
        pltpu.VMEM((HPD, 8, HD, CH), jnp.bfloat16),
        pltpu.VMEM((HPD, 4, 8, 8, CH), f),
        pltpu.VMEM((HPD, 4, 8, 8, CH), f),
        pltpu.VMEM((HPD, 4, HD, CH), f),
        pltpu.VMEM((HPD, 4, HD, CH), f),
        pltpu.VMEM((8, CH, HPD * HD), f),
        pltpu.VMEM((8, CH, HPD * HD), f),
    ]


def local_kernel(first_ref, q, d, k, v, marks, sel, o_out, dq_out, dk_out, dv_out, dm,
                 kt, vt, gates, dgates, ot, dqt, dk, dv):
    first = first_ref[0]
    ot[...] = jnp.zeros_like(ot)
    dqt[...] = jnp.zeros_like(dqt)
    dk[...] = jnp.zeros_like(dk)
    dv[...] = jnp.zeros_like(dv)
    dgates[...] = jnp.zeros_like(dgates)
    dm[...] = jnp.zeros_like(dm)

    @pl.loop(0, 4)
    def _(t):
        gate_tile(t, first, q, marks, sel, gates)

    @pl.loop(0, 8)
    def _(kc):
        transpose_chunk(kc, k, kt)
        transpose_chunk(kc, v, vt)

    args = (q, d, k, v, kt, vt, gates, dgates, ot, dqt, dk, dv)

    @pl.loop(0, 4)
    def _(t):
        cell(t, t + 4, True, *args)

        @pl.loop(t, t + 4)
        def _(kc):
            cell(t, kc, False, *args)

        close_tile(t, q, marks, gates, dgates, ot, dqt, dm, o_out, dq_out)

    @pl.loop(0, 8)
    def _(kc):
        dk_out[rows(kc), :] = (dk[kc] * SCALE).astype(jnp.bfloat16)
        dv_out[rows(kc), :] = dv[kc].astype(jnp.bfloat16)


def local_call(first, q, d, k, v, marks, sel):
    vm = pl.BlockSpec(memory_space=pltpu.VMEM)
    b = jnp.bfloat16
    return pl.pallas_call(
        local_kernel,
        out_shape=[
            jax.ShapeDtypeStruct((1024, 256), b),
            jax.ShapeDtypeStruct((1024, 256), b),
            jax.ShapeDtypeStruct((2048, 256), b),
            jax.ShapeDtypeStruct((2048, 256), b),
            jax.ShapeDtypeStruct((8, 8, 256), jnp.float32),
        ],
        in_specs=[pl.BlockSpec(memory_space=pltpu.SMEM)] + [vm] * 6,
        out_specs=[vm] * 5,
        scratch_shapes=all_scratch(),
        compiler_params=pltpu.CompilerParams(vmem_limit_bytes=56 * 1024 * 1024),
    )(first, q, d, k, v, marks, sel)


def spread(x):
    return lax.all_to_all(x, "y", split_axis=1, concat_axis=0, tiled=True)


def gathered(x):
    return spread(lax.all_to_all(x, "head", split_axis=1, concat_axis=0, tiled=True))


def returned(x):
    return lax.all_to_all(x, "y", split_axis=0, concat_axis=1, tiled=True)


def along_z(x, by):
    n = lax.axis_size("z")
    return lax.ppermute(x, "z", [(i, (i + by) % n) for i in range(n)])


def per_device(queries, keys, values, landmarks, grad_out, selections):
    k, v = gathered(keys), gathered(values)
    kp, vp = along_z(k, 1), along_z(v, 1)
    q, d = gathered(queries), gathered(grad_out)
    mk = spread(landmarks)
    mkp = along_z(mk, 1)
    marks = jnp.concatenate([mkp, mk]).astype(jnp.float32).reshape(8, CB, HPD * HD)
    marks = jnp.concatenate([marks, jnp.zeros_like(marks)], axis=1)
    sel = lax.all_gather(selections, "y").transpose(0, 2, 1)
    sel = jnp.repeat(sel, BLOCK, axis=2)
    first = (lax.axis_index("z") - 1) * 16
    o, dq, dk, dv, dm = local_call(
        first.astype(jnp.int32).reshape(1), q, d,
        jnp.concatenate([kp, k]), jnp.concatenate([vp, v]), marks, sel)
    n = q.shape[0]
    dk = dk[n:].astype(jnp.float32) + along_z(dk[:n], -1).astype(jnp.float32)
    dv = dv[n:].astype(jnp.float32) + along_z(dv[:n], -1).astype(jnp.float32)
    dm = dm[:, :CB].reshape(32, HPD * HD)
    dm = dm[16:] + along_z(dm[:16], -1)
    b = jnp.bfloat16
    return (returned(o), returned(dq), returned(dk.astype(b)), returned(dv.astype(b)),
            returned(dm).astype(b))


def solution(mesh):
    shape = (mesh.shape["seq"] // 4, 4, mesh.shape["head"])
    split = jax.sharding.Mesh(mesh.devices.reshape(shape), ("z", "y", "head"))
    rows_all = P(("z", "y", "head"), None)
    out = P(("z", "y"), "head")
    return jax.shard_map(
        per_device, mesh=split,
        in_specs=(rows_all, rows_all, rows_all, out, rows_all, P(("z", "y"), None)),
        out_specs=(out,) * 5, check_vma=False)
```

```python
import jax
import jax.numpy as jnp
from jax import lax
from jax.experimental import pallas as pl
from jax.experimental.pallas import tpu as pltpu
from jax.sharding import PartitionSpec as P

HD = 128
BLOCK = 64
HPD = 2
CH = 256
CB = CH // BLOCK
SCALE = HD ** (-0.5)
LOG2E = 1.4426950408889634
NT = (((1,), (1,)), ((), ()))
NN = (((1,), (0,)), ((), ()))
TN = (((0,), (0,)), ((), ()))


def dot(a, b, dims):
    return lax.dot_general(a, b, dims, preferred_element_type=jnp.float32)


def rows(c):
    return pl.ds(pl.multiple_of(c * CH, CH), CH)


def lanes(h):
    return slice(h * HD, (h + 1) * HD)


def gate_tile(t, first, q, marks, sel, gates):
    row = lax.broadcasted_iota(jnp.int32, (64, CH), 0)
    sub = row % 8
    block = first + (row // 8) * CB + sub
    block = jnp.where((sub < CB) & (block >= 0), block, -2)
    picks = sel[t]
    live = block == picks[0:1]
    for e in range(1, picks.shape[0]):
        live = live | (block == picks[e:e + 1])
    for h in range(HPD):
        mk = marks[:, :, lanes(h)].reshape(64, HD).astype(jnp.bfloat16)
        coarse = dot(mk, q[rows(t), lanes(h)], NT) * SCALE
        coarse = jnp.where(live, coarse, -1e30)
        top = jnp.max(coarse, axis=0, keepdims=True)
        ex = jnp.exp(coarse - top)
        gates[h, t] = (ex / jnp.sum(ex, axis=0, keepdims=True)).reshape(8, 8, CH)


def cell(t, kc, diag, q, d, k, v, kt, vt, gates, dgates, ot, dqt, dk, dv):
    for h in range(HPD):
        qh = q[rows(t), lanes(h)]
        dh = d[rows(t), lanes(h)]
        s = dot(k[rows(kc), lanes(h)], qh, NT)
        g = dot(v[rows(kc), lanes(h)], dh, NT)
        if diag:
            j = lax.broadcasted_iota(jnp.int32, (CH, CH), 0)
            i = lax.broadcasted_iota(jnp.int32, (CH, CH), 1)
            s = jnp.where(j > i, -1e30, s)
        s = s.reshape(CB, BLOCK, CH)
        g = g.reshape(CB, BLOCK, CH)
        top = jnp.max(s, axis=1, keepdims=True)
        p = jnp.exp2((s - top) * (SCALE * LOG2E))
        rz = 1.0 / jnp.sum(p, axis=1, keepdims=True)
        dg = jnp.sum(p * g, axis=1, keepdims=True) * rz
        gate = gates[h, t, kc][0:CB].reshape(CB, 1, CH)
        w = p * (gate * rz)
        ds = w * (g - dg)
        dgates[h, t, kc, 0:CB] = dg.reshape(CB, CH)
        wb = w.astype(jnp.bfloat16).reshape(CH, CH)
        sb = ds.astype(jnp.bfloat16).reshape(CH, CH)
        ot[h, t] += dot(vt[h, kc], wb, NN)
        dqt[h, t] += dot(kt[h, kc], sb, NN)
        dv[kc, :, lanes(h)] += dot(wb, dh, NN)
        dk[kc, :, lanes(h)] += dot(sb, qh, NN)


def transpose_chunk(kc, src, dst):
    for h in range(HPD):
        dst[h, kc] = src[rows(kc), lanes(h)].T


def close_tile(t, q, marks, gates, dgates, ot, dqt, dm, o_out, dq_out):
    for h in range(HPD):
        gate = gates[h, t].reshape(64, CH)
        dg = dgates[h, t].reshape(64, CH)
        dc = gate * (dg - jnp.sum(gate * dg, axis=0, keepdims=True))
        dcb = dc.astype(jnp.bfloat16)
        mk = marks[:, :, lanes(h)].reshape(64, HD).astype(jnp.bfloat16)
        dq = dqt[h, t] + dot(mk, dcb, TN)
        o_out[t, :, lanes(h)] = ot[h, t].T.astype(jnp.bfloat16)
        dq_out[t, :, lanes(h)] = (dq * SCALE).T.astype(jnp.bfloat16)
        dm[:, :, lanes(h)] += (dot(dcb, q[rows(t), lanes(h)], NN) * SCALE).reshape(8, 8, HD)


def all_scratch():
    f = jnp.float32
    return [
        pltpu.VMEM((HPD, 8, HD, CH), jnp.bfloat16),
        pltpu.VMEM((HPD, 8, HD, CH), jnp.bfloat16),
        pltpu.VMEM((HPD, 4, 8, 8, CH), f),
        pltpu.VMEM((HPD, 4, 8, 8, CH), f),
        pltpu.VMEM((HPD, 4, HD, CH), f),
        pltpu.VMEM((HPD, 4, HD, CH), f),
        pltpu.VMEM((8, CH, HPD * HD), f),
        pltpu.VMEM((8, CH, HPD * HD), f),
    ]


MESH = pl.DeviceIdType.MESH
NY = 4
K, V, Q, D = 0, 1, 2, 3


def remote(src, dst, send, recv, **where):
    return pltpu.make_async_remote_copy(
        src_ref=src, dst_ref=dst, send_sem=send, recv_sem=recv, device_id=where, device_id_type=MESH)


def kernel(nz, nh, k_in, v_in, q_in, d_in, marks_in, sel_in,
           o_out, dq_out, dk_out, dv_out, dm_out,
           xb, k_win, v_win, q_all, d_all, marks, sel, gsend, gback, osend, dm, dmback, dmsend,
           kt, vt, gates, dgates, ot, dqt, dk, dv,
           x_loc, x_send, x_recv, y_loc, y_send, y_recv, z_send, z_recv,
           s_loc, s_send, s_recv, mz_send, mz_recv, g_send, g_recv, gm_send, gm_recv,
           o_loc, o_send, o_recv):
    z, y, h = lax.axis_index("z"), lax.axis_index("y"), lax.axis_index("head")
    up, down = lax.rem(z + 1, nz), lax.rem(z + nz - 1, nz)
    inputs = (k_in, v_in, q_in, d_in)
    wide = xb.shape[2]
    part = k_in.shape[0]

    def to_y(k):
        return lax.rem(y + k, NY)

    def from_y(k):
        return lax.rem(y + NY - k, NY)

    def cols(c):
        return pl.ds(pl.multiple_of(c * CH, CH), CH)

    barrier = pltpu.get_barrier_semaphore()
    for k in range(1, nh):
        pl.semaphore_signal(barrier, inc=1, device_id={"head": lax.rem(h + k, nh)}, device_id_type=MESH)
    for k in range(1, NY):
        pl.semaphore_signal(barrier, inc=1, device_id={"y": to_y(k)}, device_id_type=MESH)
    for other in (up, down):
        pl.semaphore_signal(barrier, inc=1, device_id={"z": other}, device_id_type=MESH)
    pl.semaphore_wait(barrier, nh + NY)

    def x_copies(a):
        out = []
        mine = pl.ds(pl.multiple_of(h * part, part), part)
        for k in range(1, nh):
            to = lax.rem(h + k, nh)
            out.append(remote(
                inputs[a].at[:, pl.ds(pl.multiple_of(to * wide, wide), wide)],
                xb.at[a, mine, :], x_send.at[a, k], x_recv.at[a, k], head=to))
        return out

    def x_local(a):
        mine = pl.ds(pl.multiple_of(h * part, part), part)
        return pltpu.make_async_copy(
            inputs[a].at[:, pl.ds(pl.multiple_of(h * wide, wide), wide)], xb.at[a, mine, :], x_loc.at[a])

    def x_start(a):
        for c in x_copies(a):
            c.start()
        x_local(a).start()

    def x_wait(a):
        for c in x_copies(a):
            c.wait_recv()
        x_local(a).wait()

    def own_rows(a, c):
        if a == K:
            return k_win.at[rows(NY + c), :]
        if a == V:
            return v_win.at[rows(NY + c), :]
        return (q_all if a == Q else d_all).at[rows(c), :]

    def y_copy(a, k):
        to = to_y(k)
        return remote(xb.at[a, :, cols(to)], own_rows(a, y), y_send.at[a, k], y_recv.at[a, k], y=to)

    def y_arrival(a, k):
        return remote(xb.at[a, :, cols(y)], own_rows(a, from_y(k)), y_send.at[a, k], y_recv.at[a, k], y=y)

    def y_local(a):
        return pltpu.make_async_copy(xb.at[a, :, cols(y)], own_rows(a, y), y_loc.at[a])

    def y_start(a):
        for k in range(1, NY):
            y_copy(a, k).start()
        y_local(a).start()

    def z_copy(a, k):
        win = (k_win, v_win)[a]
        c = from_y(k)
        src = xb.at[a, :, cols(y)] if k == 0 else win.at[rows(NY + c), :]
        return remote(src, win.at[rows(c), :], z_send.at[a, k], z_recv.at[a, k], z=up)

    mark_loc = pltpu.make_async_copy(marks_in.at[:, cols(y)], marks.at[NY + y], s_loc.at[0])
    sel_loc = pltpu.make_async_copy(sel_in, sel.at[y], s_loc.at[1])

    def mark_copy(k):
        to = to_y(k)
        return remote(marks_in.at[:, cols(to)], marks.at[NY + y], s_send.at[0, k], s_recv.at[0, k], y=to)

    def mark_arrival(k):
        return remote(marks_in.at[:, cols(y)], marks.at[NY + from_y(k)], s_send.at[0, k], s_recv.at[0, k], y=y)

    def sel_copy(k):
        return remote(sel_in, sel.at[y], s_send.at[1, k], s_recv.at[1, k], y=to_y(k))

    def sel_arrival(k):
        return remote(sel_in, sel.at[from_y(k)], s_send.at[1, k], s_recv.at[1, k], y=y)

    mark_up = remote(marks.at[pl.ds(NY, NY)], marks.at[pl.ds(0, NY)], mz_send, mz_recv, z=up)

    mark_loc.start()
    sel_loc.start()
    for k in range(1, NY):
        mark_copy(k).start()
        sel_copy(k).start()
    x_start(K)
    x_start(V)

    ot[...] = jnp.zeros_like(ot)
    dqt[...] = jnp.zeros_like(dqt)
    dk[...] = jnp.zeros_like(dk)
    dv[...] = jnp.zeros_like(dv)
    dgates[...] = jnp.zeros_like(dgates)
    dm[...] = jnp.zeros_like(dm)

    mark_loc.wait()
    sel_loc.wait()
    for k in range(1, NY):
        mark_arrival(k).wait_recv()
        sel_arrival(k).wait_recv()
    mark_up.start()

    for a, following in ((K, Q), (V, D)):
        x_wait(a)
        y_start(a)
        z_copy(a, 0).start()
        x_start(following)
    for a in (K, V):
        for k in range(1, NY):
            y_arrival(a, k).wait_recv()
            z_copy(a, k).start()
        y_local(a).wait()
    mark_up.wait_recv()

    @pl.loop(NY, 2 * NY)
    def _(kc):
        transpose_chunk(kc, k_win, kt)
        transpose_chunk(kc, v_win, vt)

    x_wait(Q)
    y_start(Q)
    x_wait(D)
    y_start(D)
    for k in range(1, NY):
        y_arrival(Q, k).wait_recv()
    y_local(Q).wait()

    first = (z - 1) * (NY * CB)

    @pl.loop(0, NY)
    def _(t):
        gate_tile(t, first, q_all, marks, sel, gates)

    for k in range(1, NY):
        y_arrival(D, k).wait_recv()
    y_local(D).wait()

    args = (q_all, d_all, k_win, v_win, kt, vt, gates, dgates, ot, dqt, dk, dv)

    @pl.loop(0, NY)
    def _(c):
        cell(c, c + NY, True, *args)

        @pl.loop(c + 1, NY)
        def _(t):
            cell(t, c + NY, False, *args)

    def arrival(a, k):
        win = (k_win, v_win)[a]
        return remote(win.at[rows(NY), :], win.at[rows(from_y(k)), :], z_send.at[a, k], z_recv.at[a, k], z=up)

    def g_copy(a, k):
        c = from_y(k)
        return remote(gsend.at[a, c], gback.at[a, c], g_send.at[a, k], g_recv.at[a, k], z=down)

    @pl.loop(0, NY)
    def _(k):
        c = from_y(k)
        arrival(K, k).wait_recv()
        arrival(V, k).wait_recv()
        transpose_chunk(c, k_win, kt)
        transpose_chunk(c, v_win, vt)

        @pl.loop(0, c + 1)
        def _(t):
            cell(t, c, False, *args)

        gsend[K, c] = (dk[c] * SCALE).astype(jnp.bfloat16)
        g_copy(K, k).start()
        gsend[V, c] = dv[c].astype(jnp.bfloat16)
        g_copy(V, k).start()

    outs = (dk_out, dv_out, o_out, dq_out)

    def o_copy(a, k):
        to = from_y(k)
        return remote(osend.at[a, to], outs[a].at[:, cols(y)], o_send.at[a, k], o_recv.at[a, k], y=to)

    def o_arrival(a, k):
        return remote(osend.at[a, 0], outs[a].at[:, cols(to_y(k))], o_send.at[a, k], o_recv.at[a, k], y=y)

    def o_local(a):
        return pltpu.make_async_copy(osend.at[a, y], outs[a].at[:, cols(y)], o_loc.at[a])

    def o_start(a, k):
        if k == 0:
            o_local(a).start()
        else:
            o_copy(a, k).start()

    for k in (1, 2, 3, 0):
        t = from_y(k)
        close_tile(t, q_all, marks, gates, dgates, ot, dqt, dm, osend.at[Q], osend.at[D])
        o_start(Q, k)
        o_start(D, k)

    dmsend[...] = dm[0:NY]
    dm_back = remote(dmsend, dmback, gm_send, gm_recv, z=down)
    dm_back.start()

    for k in range(NY):
        c = from_y(k)
        g_copy(K, k).wait_recv()
        osend[K, c] = (dk[NY + c] * SCALE + gback[K, c].astype(jnp.float32)).astype(jnp.bfloat16)
        o_start(K, k)
        g_copy(V, k).wait_recv()
        osend[V, c] = (dv[NY + c] + gback[V, c].astype(jnp.float32)).astype(jnp.bfloat16)
        o_start(V, k)

    dm_back.wait_recv()
    dm[NY:] = dm[NY:] + dmback[...]

    def dm_copy(k):
        to = from_y(k)
        return remote(dm.at[NY + to], dm_out.at[:, cols(y)], o_send.at[4, k], o_recv.at[4, k], y=to)

    def dm_arrival(k):
        return remote(dm.at[NY], dm_out.at[:, cols(to_y(k))], o_send.at[4, k], o_recv.at[4, k], y=y)

    dm_local = pltpu.make_async_copy(dm.at[NY + y], dm_out.at[:, cols(y)], o_loc.at[4])
    for k in range(1, NY):
        dm_copy(k).start()
    dm_local.start()

    for a in range(4):
        for c in x_copies(a):
            c.wait_send()
        for k in range(1, NY):
            y_copy(a, k).wait_send()
            o_copy(a, k).wait_send()
            o_arrival(a, k).wait_recv()
        o_local(a).wait()
    for k in range(1, NY):
        mark_copy(k).wait_send()
        sel_copy(k).wait_send()
        dm_copy(k).wait_send()
        dm_arrival(k).wait_recv()
    dm_local.wait()
    for a in (K, V):
        for k in range(NY):
            z_copy(a, k).wait_send()
            g_copy(a, k).wait_send()
    mark_up.wait_send()
    dm_back.wait_send()


def per_device(queries, keys, values, landmarks, grad_out, selections):
    nz, nh = lax.axis_size("z"), lax.axis_size("head")
    width = landmarks.shape[1]
    marks = jnp.concatenate([landmarks.astype(jnp.float32), jnp.zeros((8 - CB, width), jnp.float32)])
    sel = jnp.repeat(selections.T, BLOCK, axis=1)
    b, f = jnp.bfloat16, jnp.float32
    hbm = pl.BlockSpec(memory_space=pl.ANY)
    big = jax.ShapeDtypeStruct((CH, width), b)
    tall = NY * CH
    feat = HPD * HD
    sem = pltpu.SemaphoreType.DMA
    o, dq, dk, dv, dm = pl.pallas_call(
        lambda *refs: kernel(nz, nh, *refs),
        out_shape=[big] * 4 + [jax.ShapeDtypeStruct((8, width), f)],
        in_specs=[hbm] * 6,
        out_specs=[hbm] * 5,
        scratch_shapes=[
            pltpu.VMEM((4, CH, width), b),
            pltpu.VMEM((2 * tall, feat), b),
            pltpu.VMEM((2 * tall, feat), b),
            pltpu.VMEM((tall, feat), b),
            pltpu.VMEM((tall, feat), b),
            pltpu.VMEM((8, 8, feat), f),
            pltpu.VMEM((NY, selections.shape[1], CH), jnp.int32),
            pltpu.VMEM((2, NY, CH, feat), b),
            pltpu.VMEM((2, NY, CH, feat), b),
            pltpu.VMEM((4, NY, CH, feat), b),
            pltpu.VMEM((8, 8, feat), f),
            pltpu.VMEM((NY, 8, feat), f),
            pltpu.VMEM((NY, 8, feat), f),
        ] + all_scratch() + [
            sem((4,)), sem((4, 8)), sem((4, 8)),
            sem((4,)), sem((4, 4)), sem((4, 4)),
            sem((2, 4)), sem((2, 4)),
            sem((2,)), sem((2, 4)), sem((2, 4)),
            sem, sem,
            sem((2, 4)), sem((2, 4)), sem, sem,
            sem((5,)), sem((5, 4)), sem((5, 4)),
        ],
        compiler_params=pltpu.CompilerParams(
            collective_id=0, has_side_effects=True, vmem_limit_bytes=48 * 1024 * 1024),
    )(keys, values, queries, grad_out, marks, sel)
    return o, dq, dk, dv, dm[:CB].astype(b)


def solution(mesh):
    shape = (mesh.shape["seq"] // NY, NY, mesh.shape["head"])
    split = jax.sharding.Mesh(mesh.devices.reshape(shape), ("z", "y", "head"))
    rows_all = P(("z", "y", "head"), None)
    out = P(("z", "y"), "head")
    return jax.shard_map(
        per_device, mesh=split,
        in_specs=(rows_all, rows_all, rows_all, out, rows_all, P(("z", "y"), None)),
        out_specs=(out,) * 5, check_vma=False)
```

```python
import jax
import jax.numpy as jnp
from jax import lax
from jax.experimental import pallas as pl
from jax.experimental.pallas import tpu as pltpu
from jax.sharding import PartitionSpec as P

HD = 128
BLOCK = 64
HPD = 2
CH = 256
CB = CH // BLOCK
NY = 4
SCALE = HD ** (-0.5)
LOG2E = 1.4426950408889634
NT = (((1,), (1,)), ((), ()))
NN = (((1,), (0,)), ((), ()))
TN = (((0,), (0,)), ((), ()))
MESH = pl.DeviceIdType.MESH
K, V, Q, D = 0, 1, 2, 3


def dot(a, b, dims):
    return lax.dot_general(a, b, dims, preferred_element_type=jnp.float32)


def rows(c):
    return pl.ds(pl.multiple_of(c * CH, CH), CH)


def gate_tile(s, t, first, q, marks, sel, gates):
    row = lax.broadcasted_iota(jnp.int32, (64, CH), 0)
    sub = row % 8
    block = first + (row // 8) * CB + sub
    block = jnp.where((sub < CB) & (block >= 0), block, -2).astype(jnp.float32)
    picks = sel[t]
    live = block == picks[0:1]
    for e in range(1, picks.shape[0]):
        live = live | (block == picks[e:e + 1])
    mk = marks[:, :, s * HD:(s + 1) * HD].reshape(64, HD).astype(jnp.bfloat16)
    coarse = dot(mk, q[s, rows(t), :], NT) * SCALE
    coarse = jnp.where(live, coarse, -1e30)
    top = jnp.max(coarse, axis=0, keepdims=True)
    ex = jnp.exp(coarse - top)
    gates[s, t] = (ex / jnp.sum(ex, axis=0, keepdims=True)).reshape(8, 8, CH)


def chunk_cells(h, c, q, d, k, v, kt, vt, gates, dgates, ot, dqt, dk, dv):
    cells = [(t, jnp.where(t <= c, c, c + NY), False) for t in range(NY)] + [(c, c + NY, True)]

    def first(i):
        t, kc, _ = cells[i]
        return (dot(k[h, rows(kc), :], q[h, rows(t), :], NT), dot(v[h, rows(kc), :], d[h, rows(t), :], NT))

    def middle(i, s, g):
        t, kc, diag = cells[i]
        if diag:
            row = lax.broadcasted_iota(jnp.int32, (CH, CH), 0)
            col = lax.broadcasted_iota(jnp.int32, (CH, CH), 1)
            s = jnp.where(row > col, -1e30, s)
        s = s.reshape(CB, BLOCK, CH)
        g = g.reshape(CB, BLOCK, CH)
        top = jnp.max(s, axis=1, keepdims=True)
        p = jnp.exp2((s - top) * (SCALE * LOG2E))
        rz = 1.0 / jnp.sum(p, axis=1, keepdims=True)
        dg = jnp.sum(p * g, axis=1, keepdims=True) * rz
        gate = gates[h, t, kc][0:CB].reshape(CB, 1, CH)
        w = p * (gate * rz)
        ds = w * (g - dg)
        dgates[h, t, kc, 0:CB] = dg.reshape(CB, CH)
        return w.astype(jnp.bfloat16).reshape(CH, CH), ds.astype(jnp.bfloat16).reshape(CH, CH)

    def last(i, wb, sb):
        t, kc, _ = cells[i]
        ot[h, t] += dot(vt[h, kc], wb, NN)
        dqt[h, t] += dot(kt[h, kc], sb, NN)
        dv[h, kc] += dot(wb, d[h, rows(t), :], NN)
        dk[h, kc] += dot(sb, q[h, rows(t), :], NN)

    ready, done = first(0), None
    for i in range(len(cells)):
        following = first(i + 1) if i + 1 < len(cells) else None
        pair = middle(i, *ready)
        if done is not None:
            last(i - 1, *done)
        ready, done = following, pair
    last(len(cells) - 1, *done)


def close_tile(s, t, q, marks, gates, dgates, ot, dqt, dm, osend):
    gate = gates[s, t].reshape(64, CH)
    dg = dgates[s, t].reshape(64, CH)
    dc = gate * (dg - jnp.sum(gate * dg, axis=0, keepdims=True))
    dcb = dc.astype(jnp.bfloat16)
    mk = marks[:, :, s * HD:(s + 1) * HD].reshape(64, HD).astype(jnp.bfloat16)
    dq = dqt[s, t] + dot(mk, dcb, TN)
    osend[Q, s, t] = ot[s, t].T.astype(jnp.bfloat16)
    osend[D, s, t] = (dq * SCALE).T.astype(jnp.bfloat16)
    dm[:, :, s * HD:(s + 1) * HD] += (dot(dcb, q[s, rows(t), :], NN) * SCALE).reshape(8, 8, HD)


def remote(src, dst, send, recv, **where):
    return pltpu.make_async_remote_copy(
        src_ref=src, dst_ref=dst, send_sem=send, recv_sem=recv, device_id=where, device_id_type=MESH)


def kernel(nz, nh, k_in, v_in, q_in, d_in, marks_in, sel_in,
           dk_out, dv_out, o_out, dq_out, dm_out,
           xb, k_win, v_win, q_all, d_all, marks_own, sel_own, marks, sel, gsend, gback, osend, dm, dmback, dmsend,
           kt, vt, gates, dgates, ot, dqt, dk, dv,
           x_loc, x_send, x_recv, y_loc, y_send, y_recv, z_send, z_recv,
           s_loc, s_send, s_recv, mz_send, mz_recv, g_send, g_recv, gm_send, gm_recv,
           o_loc, o_send, o_recv):
    z, y, h = lax.axis_index("z"), lax.axis_index("y"), lax.axis_index("head")
    up, down = lax.rem(z + 1, nz), lax.rem(z + nz - 1, nz)
    inputs = (k_in, v_in, q_in, d_in)
    outs = (dk_out, dv_out, o_out, dq_out)
    part = k_in.shape[0]
    half = NY * HD
    wide = HPD * half
    mine = pl.ds(pl.multiple_of(h * part, part), part)

    def to_y(k):
        return lax.rem(y + k, NY)

    def from_y(k):
        return lax.rem(y + NY - k, NY)

    def cols(c, n=HD, base=0):
        return pl.ds(pl.multiple_of(base + c * n, HD), n)

    barrier = pltpu.get_barrier_semaphore()
    for k in range(1, nh):
        pl.semaphore_signal(barrier, inc=1, device_id={"head": lax.rem(h + k, nh)}, device_id_type=MESH)
    for k in range(1, NY):
        pl.semaphore_signal(barrier, inc=1, device_id={"y": to_y(k)}, device_id_type=MESH)
    for other in (up, down):
        pl.semaphore_signal(barrier, inc=1, device_id={"z": other}, device_id_type=MESH)
    pl.semaphore_wait(barrier, nh + NY)

    def x_copies(s, a):
        out = []
        for k in range(1, nh):
            to = lax.rem(h + k, nh)
            out.append(remote(
                inputs[a].at[:, pl.ds(pl.multiple_of(to * wide + s * half, half), half)],
                xb.at[s, a, mine, :], x_send.at[4 * s + a, k], x_recv.at[4 * s + a, k], head=to))
        return out

    def x_local(s, a):
        return pltpu.make_async_copy(
            inputs[a].at[:, pl.ds(pl.multiple_of(h * wide + s * half, half), half)],
            xb.at[s, a, mine, :], x_loc.at[4 * s + a])

    def x_start(s, a):
        for c in x_copies(s, a):
            c.start()
        x_local(s, a).start()

    def x_wait(s, a):
        for c in x_copies(s, a):
            c.wait_recv()
        x_local(s, a).wait()

    def own_rows(s, a, c):
        if a == K:
            return k_win.at[s, rows(NY + c), :]
        if a == V:
            return v_win.at[s, rows(NY + c), :]
        return (q_all if a == Q else d_all).at[s, rows(c), :]

    def y_copy(s, a, k):
        to = to_y(k)
        return remote(xb.at[s, a, :, cols(to)], own_rows(s, a, y),
                      y_send.at[4 * s + a, k], y_recv.at[4 * s + a, k], y=to)

    def y_arrival(s, a, k):
        return remote(xb.at[s, a, :, cols(y)], own_rows(s, a, from_y(k)),
                      y_send.at[4 * s + a, k], y_recv.at[4 * s + a, k], y=to_y(k))

    def y_local(s, a):
        return pltpu.make_async_copy(xb.at[s, a, :, cols(y)], own_rows(s, a, y), y_loc.at[4 * s + a])

    def y_start(s, a):
        for k in range(1, NY):
            y_copy(s, a, k).start()
        y_local(s, a).start()

    def y_wait(s, a):
        for k in range(1, NY):
            y_arrival(s, a, k).wait_recv()
        y_local(s, a).wait()

    def z_copy(s, a, k):
        win = (k_win, v_win)[a]
        c = from_y(k)
        src = xb.at[s, a, :, cols(y)] if k == 0 else win.at[s, rows(NY + c), :]
        return remote(src, win.at[s, rows(c), :], z_send.at[2 * s + a, k], z_recv.at[2 * s + a, k], z=up)

    def z_pass(s, a):
        for k in range(1, NY):
            y_arrival(s, a, k).wait_recv()
            z_copy(s, a, k).start()
        y_local(s, a).wait()

    feat = HPD * HD
    mark_loc = pltpu.make_async_copy(marks_own.at[y], marks.at[NY + y], s_loc.at[0])
    sel_loc = pltpu.make_async_copy(sel_own, sel.at[y], s_loc.at[1])

    def mark_copy(k):
        to = to_y(k)
        return remote(marks_own.at[to], marks.at[NY + y], s_send.at[0, k], s_recv.at[0, k], y=to)

    def mark_arrival(k):
        return remote(marks_own.at[y], marks.at[NY + from_y(k)],
                      s_send.at[0, k], s_recv.at[0, k], y=to_y(k))

    def sel_copy(k):
        return remote(sel_own, sel.at[y], s_send.at[1, k], s_recv.at[1, k], y=to_y(k))

    def sel_arrival(k):
        return remote(sel_own, sel.at[from_y(k)], s_send.at[1, k], s_recv.at[1, k], y=to_y(k))

    mark_up = remote(marks.at[pl.ds(NY, NY)], marks.at[pl.ds(0, NY)], mz_send, mz_recv, z=up)

    args = (q_all, d_all, k_win, v_win, kt, vt, gates, dgates, ot, dqt, dk, dv)
    first = (z - 1) * (NY * CB)

    def transpose_chunk(s, kc):
        kt[s, kc] = k_win[s, rows(kc), :].T
        vt[s, kc] = v_win[s, rows(kc), :].T

    def g_copy(s, a, k):
        c = from_y(k)
        return remote(gsend.at[a, s, c], gback.at[a, s, c], g_send.at[2 * s + a, k], g_recv.at[2 * s + a, k], z=down)

    def prepare(s):
        @pl.loop(0, NY)
        def _(t):
            gate_tile(s, t, first, q_all, marks, sel, gates)

    def chunk(s, k):
        c = from_y(k)
        z_copy(s, K, k).wait_recv()
        z_copy(s, V, k).wait_recv()
        transpose_chunk(s, c)
        transpose_chunk(s, c + NY)
        chunk_cells(s, c, *args)
        gsend[K, s, c] = (dk[s, c] * SCALE).astype(jnp.bfloat16)
        g_copy(s, K, k).start()
        gsend[V, s, c] = dv[s, c].astype(jnp.bfloat16)
        g_copy(s, V, k).start()

    def o_copy(s, a, k):
        to = from_y(k)
        return remote(osend.at[a, s, to], outs[a].at[:, cols(y, HD, s * half)],
                      o_send.at[4 * s + a, k], o_recv.at[4 * s + a, k], y=to)

    def o_arrival(s, a, k):
        return remote(osend.at[a, s, 0], outs[a].at[:, cols(to_y(k), HD, s * half)],
                      o_send.at[4 * s + a, k], o_recv.at[4 * s + a, k], y=to_y(k))

    def o_local(s, a):
        return pltpu.make_async_copy(osend.at[a, s, y], outs[a].at[:, cols(y, HD, s * half)], o_loc.at[4 * s + a])

    def o_start(s, a, k):
        if k == 0:
            o_local(s, a).start()
        else:
            o_copy(s, a, k).start()

    def close(s):
        for k in (1, 2, 3, 0):
            close_tile(s, from_y(k), q_all, marks, gates, dgates, ot, dqt, dm, osend)
            o_start(s, Q, k)
            o_start(s, D, k)

    def finish(s):
        for k in range(NY):
            c = from_y(k)
            g_copy(s, K, k).wait_recv()
            osend[K, s, c] = (dk[s, NY + c] * SCALE + gback[K, s, c].astype(jnp.float32)).astype(jnp.bfloat16)
            o_start(s, K, k)
            g_copy(s, V, k).wait_recv()
            osend[V, s, c] = (dv[s, NY + c] + gback[V, s, c].astype(jnp.float32)).astype(jnp.bfloat16)
            o_start(s, V, k)

    x_start(0, K)
    x_start(0, V)
    x_start(0, Q)
    for to in range(NY):
        for s in range(HPD):
            part_of = marks_in[:, s * half + to * HD:s * half + (to + 1) * HD].astype(jnp.float32)
            marks_own[to, :, s * HD:(s + 1) * HD] = jnp.concatenate([part_of, jnp.zeros((8 - CB, HD), jnp.float32)])
    row = lax.broadcasted_iota(jnp.int32, (CB, CH), 0)
    col = lax.broadcasted_iota(jnp.int32, (CB, CH), 1)
    of_block = (col // BLOCK == row).astype(jnp.bfloat16)
    sel_own[...] = dot(sel_in[...].astype(jnp.float32).astype(jnp.bfloat16), of_block, TN)
    mark_loc.start()
    sel_loc.start()
    for k in range(1, NY):
        mark_copy(k).start()
        sel_copy(k).start()

    ot[...] = jnp.zeros_like(ot)
    dqt[...] = jnp.zeros_like(dqt)
    dk[...] = jnp.zeros_like(dk)
    dv[...] = jnp.zeros_like(dv)
    dgates[...] = jnp.zeros_like(dgates)
    dm[...] = jnp.zeros_like(dm)

    x_wait(0, K)
    y_start(0, K)
    z_copy(0, K, 0).start()
    x_start(0, D)
    x_wait(0, V)
    y_start(0, V)
    z_copy(0, V, 0).start()
    x_start(1, K)
    mark_loc.wait()
    sel_loc.wait()
    for k in range(1, NY):
        mark_arrival(k).wait_recv()
        sel_arrival(k).wait_recv()
    mark_up.start()
    z_pass(0, K)
    x_wait(0, Q)
    y_start(0, Q)
    x_start(1, V)
    z_pass(0, V)
    x_wait(0, D)
    y_start(0, D)
    x_start(1, Q)
    x_wait(1, K)
    y_start(1, K)
    z_copy(1, K, 0).start()
    x_start(1, D)
    y_wait(0, Q)
    mark_up.wait_recv()
    prepare(0)
    x_wait(1, V)
    y_start(1, V)
    z_copy(1, V, 0).start()
    y_wait(0, D)
    chunk(0, 0)
    z_pass(1, K)
    chunk(0, 1)
    z_pass(1, V)
    chunk(0, 2)
    x_wait(1, Q)
    y_start(1, Q)
    chunk(0, 3)
    x_wait(1, D)
    y_start(1, D)
    close(0)
    y_wait(1, Q)
    prepare(1)
    y_wait(1, D)
    for k in range(NY):
        chunk(1, k)
    finish(0)
    close(1)

    dmsend[...] = dm[0:NY]
    dm_back = remote(dmsend, dmback, gm_send, gm_recv, z=down)
    dm_back.start()
    finish(1)
    dm_back.wait_recv()
    dm[NY:] = dm[NY:] + dmback[...]

    def dm_copy(k):
        to = from_y(k)
        return remote(dm.at[NY + to], dm_out.at[:, cols(y, feat)], s_send.at[2, k], s_recv.at[2, k], y=to)

    def dm_arrival(k):
        return remote(dm.at[NY], dm_out.at[:, cols(to_y(k), feat)], s_send.at[2, k], s_recv.at[2, k], y=to_y(k))

    dm_local = pltpu.make_async_copy(dm.at[NY + y], dm_out.at[:, cols(y, feat)], s_loc.at[2])
    for k in range(1, NY):
        dm_copy(k).start()
    dm_local.start()

    for s in range(HPD):
        for a in range(4):
            for c in x_copies(s, a):
                c.wait_send()
            for k in range(1, NY):
                y_copy(s, a, k).wait_send()
                o_copy(s, a, k).wait_send()
                o_arrival(s, a, k).wait_recv()
            o_local(s, a).wait()
        for a in (K, V):
            for k in range(NY):
                z_copy(s, a, k).wait_send()
                g_copy(s, a, k).wait_send()
    for k in range(1, NY):
        mark_copy(k).wait_send()
        sel_copy(k).wait_send()
        dm_copy(k).wait_send()
        dm_arrival(k).wait_recv()
    dm_local.wait()
    mark_up.wait_send()
    dm_back.wait_send()


def hand_over(*refs):
    for n in range(4):
        refs[5 + n][...] = refs[n][...]
    for y in range(NY):
        for s in range(HPD):
            to = (s * NY + y) * HD
            at = (y * HPD + s) * HD
            refs[9][:, to:to + HD] = refs[4][0:CB, at:at + HD].astype(jnp.bfloat16)


def per_device(queries, keys, values, landmarks, grad_out, selections):
    nz, nh = lax.axis_size("z"), lax.axis_size("head")
    width = landmarks.shape[1]
    b, f = jnp.bfloat16, jnp.float32
    hbm, vmem = pl.BlockSpec(memory_space=pl.ANY), pl.BlockSpec(memory_space=pltpu.VMEM)
    big = jax.ShapeDtypeStruct((CH, width), b)
    tall = NY * CH
    feat = HPD * HD
    sem = pltpu.SemaphoreType.DMA
    dk, dv, o, dq, dm = pl.pallas_call(
        lambda *refs: kernel(nz, nh, *refs),
        out_shape=[big] * 4 + [jax.ShapeDtypeStruct((8, width), f)],
        in_specs=[hbm] * 4 + [vmem] * 2,
        out_specs=[hbm] * 4 + [hbm],
        scratch_shapes=[
            pltpu.VMEM((HPD, 4, CH, NY * HD), b),
            pltpu.VMEM((HPD, 2 * tall, HD), b),
            pltpu.VMEM((HPD, 2 * tall, HD), b),
            pltpu.VMEM((HPD, tall, HD), b),
            pltpu.VMEM((HPD, tall, HD), b),
            pltpu.VMEM((NY, 8, feat), f),
            pltpu.VMEM((selections.shape[1], CH), f),
            pltpu.VMEM((8, 8, feat), f),
            pltpu.VMEM((NY, selections.shape[1], CH), f),
            pltpu.VMEM((2, HPD, NY, CH, HD), b),
            pltpu.VMEM((2, HPD, NY, CH, HD), b),
            pltpu.VMEM((4, HPD, NY, CH, HD), b),
            pltpu.VMEM((8, 8, feat), f),
            pltpu.VMEM((NY, 8, feat), f),
            pltpu.VMEM((NY, 8, feat), f),
            pltpu.VMEM((HPD, 8, HD, CH), b),
            pltpu.VMEM((HPD, 8, HD, CH), b),
            pltpu.VMEM((HPD, NY, 8, 8, CH), f),
            pltpu.VMEM((HPD, NY, 8, 8, CH), f),
            pltpu.VMEM((HPD, NY, HD, CH), f),
            pltpu.VMEM((HPD, NY, HD, CH), f),
            pltpu.VMEM((HPD, 8, CH, HD), f),
            pltpu.VMEM((HPD, 8, CH, HD), f),
            sem((8,)), sem((8, 8)), sem((8, 8)),
            sem((8,)), sem((8, 4)), sem((8, 4)),
            sem((4, 4)), sem((4, 4)),
            sem((3,)), sem((3, 4)), sem((3, 4)),
            sem, sem,
            sem((4, 4)), sem((4, 4)), sem, sem,
            sem((8,)), sem((8, 4)), sem((8, 4)),
        ],
        compiler_params=pltpu.CompilerParams(
            collective_id=0, has_side_effects=True, vmem_limit_bytes=63 * 1024 * 1024),
    )(keys, values, queries, grad_out, landmarks, selections)
    piece = pl.BlockSpec((CH // 4, width), lambda n: (n, 0))
    return pl.pallas_call(
        hand_over,
        grid=(4,),
        out_shape=[big] * 4 + [jax.ShapeDtypeStruct((CB, width), b)],
        in_specs=[piece] * 4 + [pl.BlockSpec((8, width), lambda n: (0, 0))],
        out_specs=[piece] * 4 + [pl.BlockSpec((CB, width), lambda n: (0, 0))],
        compiler_params=pltpu.CompilerParams(vmem_limit_bytes=60 * 1024 * 1024),
    )(o, dq, dk, dv, dm)


def solution(mesh):
    shape = (mesh.shape["seq"] // NY, NY, mesh.shape["head"])
    split = jax.sharding.Mesh(mesh.devices.reshape(shape), ("z", "y", "head"))
    rows_all = P(("z", "y", "head"), None)
    out = P(("z", "y"), "head")
    return jax.shard_map(
        per_device, mesh=split,
        in_specs=(rows_all, rows_all, rows_all, out, rows_all, P(("z", "y"), None)),
        out_specs=(out,) * 5, check_vma=False)
```

```python
import jax
import jax.numpy as jnp
from jax import lax
from jax.experimental import pallas as pl
from jax.experimental.pallas import tpu as pltpu
from jax.sharding import PartitionSpec as P

HD = 128
BLOCK = 64
HPD = 2
CH = 256
CB = CH // BLOCK
NY = 4
SCALE = HD ** (-0.5)
LOG2E = 1.4426950408889634
NT = (((1,), (1,)), ((), ()))
NN = (((1,), (0,)), ((), ()))
TN = (((0,), (0,)), ((), ()))
MESH = pl.DeviceIdType.MESH
K, V, Q, D = 0, 1, 2, 3


def dot(a, b, dims):
    return lax.dot_general(a, b, dims, preferred_element_type=jnp.float32)


def rows(c):
    return pl.ds(pl.multiple_of(c * CH, CH), CH)


def gate_tile(s, t, first, q, marks, sel, gates):
    row = lax.broadcasted_iota(jnp.int32, (64, CH), 0)
    sub = row % 8
    block = first + (row // 8) * CB + sub
    block = jnp.where((sub < CB) & (block >= 0), block, -2).astype(jnp.float32)
    picks = sel[t]
    live = block == picks[0:1]
    for e in range(1, picks.shape[0]):
        live = live | (block == picks[e:e + 1])
    mk = marks[:, :, s * HD:(s + 1) * HD].reshape(64, HD).astype(jnp.bfloat16)
    coarse = dot(mk, q[s, rows(t), :], NT) * SCALE
    coarse = jnp.where(live, coarse, -1e30)
    top = jnp.max(coarse, axis=0, keepdims=True)
    ex = jnp.exp(coarse - top)
    gates[s, t] = (ex / jnp.sum(ex, axis=0, keepdims=True)).reshape(8, 8, CH)


def chunk_cells(h, c, q, d, k, v, kt, vt, gates, dgates, ot, dqt, dk, dv):
    cells = [(t, jnp.where(t <= c, c, c + NY), False) for t in range(NY)] + [(c, c + NY, True)]

    def first(i):
        t, kc, _ = cells[i]
        return (dot(k[h, rows(kc), :], q[h, rows(t), :], NT), dot(v[h, rows(kc), :], d[h, rows(t), :], NT))

    def middle(i, s, g):
        t, kc, diag = cells[i]
        if diag:
            row = lax.broadcasted_iota(jnp.int32, (CH, CH), 0)
            col = lax.broadcasted_iota(jnp.int32, (CH, CH), 1)
            s = jnp.where(row > col, -1e30, s)
        s = s.reshape(CB, BLOCK, CH)
        g = g.reshape(CB, BLOCK, CH)
        top = jnp.max(s, axis=1, keepdims=True)
        p = jnp.exp2((s - top) * (SCALE * LOG2E))
        rz = 1.0 / jnp.sum(p, axis=1, keepdims=True)
        dg = jnp.sum(p * g, axis=1, keepdims=True) * rz
        gate = gates[h, t, kc][0:CB].reshape(CB, 1, CH)
        w = p * (gate * rz)
        ds = w * (g - dg)
        dgates[h, t, kc, 0:CB] = dg.reshape(CB, CH)
        return w.astype(jnp.bfloat16).reshape(CH, CH), ds.astype(jnp.bfloat16).reshape(CH, CH)

    def last(i, wb, sb):
        t, kc, _ = cells[i]
        ot[h, t] += dot(vt[h, kc], wb, NN)
        dqt[h, t] += dot(kt[h, kc], sb, NN)
        dv[h, kc] += dot(wb, d[h, rows(t), :], NN)
        dk[h, kc] += dot(sb, q[h, rows(t), :], NN)

    ready, done = first(0), None
    for i in range(len(cells)):
        following = first(i + 1) if i + 1 < len(cells) else None
        pair = middle(i, *ready)
        if done is not None:
            last(i - 1, *done)
        ready, done = following, pair
    last(len(cells) - 1, *done)


def close_tile(s, t, q, marks, gates, dgates, ot, dqt, dm, osend):
    gate = gates[s, t].reshape(64, CH)
    dg = dgates[s, t].reshape(64, CH)
    dc = gate * (dg - jnp.sum(gate * dg, axis=0, keepdims=True))
    dcb = dc.astype(jnp.bfloat16)
    mk = marks[:, :, s * HD:(s + 1) * HD].reshape(64, HD).astype(jnp.bfloat16)
    dq = dqt[s, t] + dot(mk, dcb, TN)
    osend[Q, s, t] = ot[s, t].T.astype(jnp.bfloat16)
    osend[D, s, t] = (dq * SCALE).T.astype(jnp.bfloat16)
    dm[:, :, s * HD:(s + 1) * HD] += (dot(dcb, q[s, rows(t), :], NN) * SCALE).reshape(8, 8, HD)


def remote(src, dst, send, recv, **where):
    return pltpu.make_async_remote_copy(
        src_ref=src, dst_ref=dst, send_sem=send, recv_sem=recv, device_id=where, device_id_type=MESH)


def kernel(nz, nh, k_in, v_in, q_in, d_in, marks_in, sel_in,
           dk_out, dv_out, o_out, dq_out, dm_out,
           xb, k_win, v_win, q_all, d_all, marks_own, sel_own, marks, sel, gsend, gback, osend, dm, dmback, dmsend,
           kt, vt, gates, dgates, ot, dqt, dk, dv,
           x_loc, x_send, x_recv, y_loc, y_send, y_recv, z_send, z_recv,
           s_loc, s_send, s_recv, mz_send, mz_recv, g_send, g_recv, gm_send, gm_recv,
           o_loc, o_send, o_recv):
    z, y, h = lax.axis_index("z"), lax.axis_index("y"), lax.axis_index("head")
    up, down = lax.rem(z + 1, nz), lax.rem(z + nz - 1, nz)
    inputs = (k_in, v_in, q_in, d_in)
    outs = (dk_out, dv_out, o_out, dq_out)
    part = k_in.shape[0]
    half = NY * HD
    wide = HPD * half
    mine = pl.ds(pl.multiple_of(h * part, part), part)

    def to_y(k):
        return lax.rem(y + k, NY)

    def from_y(k):
        return lax.rem(y + NY - k, NY)

    def cols(c, n=HD, base=0):
        return pl.ds(pl.multiple_of(base + c * n, HD), n)

    barrier = pltpu.get_barrier_semaphore()
    for k in range(1, nh):
        pl.semaphore_signal(barrier, inc=1, device_id={"head": lax.rem(h + k, nh)}, device_id_type=MESH)
    for k in range(1, NY):
        pl.semaphore_signal(barrier, inc=1, device_id={"y": to_y(k)}, device_id_type=MESH)
    for other in (up, down):
        pl.semaphore_signal(barrier, inc=1, device_id={"z": other}, device_id_type=MESH)
    pl.semaphore_wait(barrier, nh + NY)

    def x_copies(s, a):
        out = []
        for k in range(1, nh):
            to = lax.rem(h + k, nh)
            out.append(remote(
                inputs[a].at[:, pl.ds(pl.multiple_of(to * wide + s * half, half), half)],
                xb.at[s, a, mine, :], x_send.at[4 * s + a, k], x_recv.at[4 * s + a, k], head=to))
        return out

    def x_local(s, a):
        return pltpu.make_async_copy(
            inputs[a].at[:, pl.ds(pl.multiple_of(h * wide + s * half, half), half)],
            xb.at[s, a, mine, :], x_loc.at[4 * s + a])

    def x_start(s, a):
        for c in x_copies(s, a):
            c.start()
        x_local(s, a).start()

    def x_wait(s, a):
        for c in x_copies(s, a):
            c.wait_recv()
        x_local(s, a).wait()

    def own_rows(s, a, c):
        if a == K:
            return k_win.at[s, rows(NY + c), :]
        if a == V:
            return v_win.at[s, rows(NY + c), :]
        return (q_all if a == Q else d_all).at[s, rows(c), :]

    def y_copy(s, a, k):
        to = to_y(k)
        return remote(xb.at[s, a, :, cols(to)], own_rows(s, a, y),
                      y_send.at[4 * s + a, k], y_recv.at[4 * s + a, k], y=to)

    def y_arrival(s, a, k):
        return remote(xb.at[s, a, :, cols(y)], own_rows(s, a, from_y(k)),
                      y_send.at[4 * s + a, k], y_recv.at[4 * s + a, k], y=to_y(k))

    def y_local(s, a):
        return pltpu.make_async_copy(xb.at[s, a, :, cols(y)], own_rows(s, a, y), y_loc.at[4 * s + a])

    def y_start(s, a):
        for k in range(1, NY):
            y_copy(s, a, k).start()
        y_local(s, a).start()

    def y_wait(s, a):
        for k in range(1, NY):
            y_arrival(s, a, k).wait_recv()
        y_local(s, a).wait()

    def z_copy(s, a, k):
        win = (k_win, v_win)[a]
        c = from_y(k)
        src = xb.at[s, a, :, cols(y)] if k == 0 else win.at[s, rows(NY + c), :]
        return remote(src, win.at[s, rows(c), :], z_send.at[2 * s + a, k], z_recv.at[2 * s + a, k], z=up)

    def z_pass(s, a):
        for k in range(1, NY):
            y_arrival(s, a, k).wait_recv()
            z_copy(s, a, k).start()
        y_local(s, a).wait()

    feat = HPD * HD
    mark_loc = pltpu.make_async_copy(marks_own.at[y], marks.at[NY + y], s_loc.at[0])
    sel_loc = pltpu.make_async_copy(sel_own, sel.at[y], s_loc.at[1])

    def mark_copy(k):
        to = to_y(k)
        return remote(marks_own.at[to], marks.at[NY + y], s_send.at[0, k], s_recv.at[0, k], y=to)

    def mark_arrival(k):
        return remote(marks_own.at[y], marks.at[NY + from_y(k)],
                      s_send.at[0, k], s_recv.at[0, k], y=to_y(k))

    def sel_copy(k):
        return remote(sel_own, sel.at[y], s_send.at[1, k], s_recv.at[1, k], y=to_y(k))

    def sel_arrival(k):
        return remote(sel_own, sel.at[from_y(k)], s_send.at[1, k], s_recv.at[1, k], y=to_y(k))

    mark_up = remote(marks.at[pl.ds(NY, NY)], marks.at[pl.ds(0, NY)], mz_send, mz_recv, z=up)

    args = (q_all, d_all, k_win, v_win, kt, vt, gates, dgates, ot, dqt, dk, dv)
    first = (z - 1) * (NY * CB)

    def transpose_chunk(s, kc):
        kt[s, kc] = k_win[s, rows(kc), :].T
        vt[s, kc] = v_win[s, rows(kc), :].T

    def g_copy(s, a, k):
        c = from_y(k)
        return remote(gsend.at[a, s, c], gback.at[a, s, c], g_send.at[2 * s + a, k], g_recv.at[2 * s + a, k], z=down)

    def prepare(s):
        @pl.loop(0, NY)
        def _(t):
            gate_tile(s, t, first, q_all, marks, sel, gates)

    def chunk(s, k):
        c = from_y(k)
        z_copy(s, K, k).wait_recv()
        z_copy(s, V, k).wait_recv()
        transpose_chunk(s, c)
        transpose_chunk(s, c + NY)
        chunk_cells(s, c, *args)
        gsend[K, s, c] = (dk[s, c] * SCALE).astype(jnp.bfloat16)
        g_copy(s, K, k).start()
        gsend[V, s, c] = dv[s, c].astype(jnp.bfloat16)
        g_copy(s, V, k).start()

    def o_copy(s, a, k):
        to = from_y(k)
        return remote(osend.at[a, s, to], outs[a].at[:, cols(y, HD, s * half)],
                      o_send.at[4 * s + a, k], o_recv.at[4 * s + a, k], y=to)

    def o_arrival(s, a, k):
        return remote(osend.at[a, s, 0], outs[a].at[:, cols(to_y(k), HD, s * half)],
                      o_send.at[4 * s + a, k], o_recv.at[4 * s + a, k], y=to_y(k))

    def o_local(s, a):
        return pltpu.make_async_copy(osend.at[a, s, y], outs[a].at[:, cols(y, HD, s * half)], o_loc.at[4 * s + a])

    def o_start(s, a, k):
        if k == 0:
            o_local(s, a).start()
        else:
            o_copy(s, a, k).start()

    def close(s):
        for k in (1, 2, 3, 0):
            close_tile(s, from_y(k), q_all, marks, gates, dgates, ot, dqt, dm, osend)
            o_start(s, Q, k)
            o_start(s, D, k)

    def finish(s, turns):
        for k in turns:
            c = from_y(k)
            g_copy(s, K, k).wait_recv()
            osend[K, s, c] = (dk[s, NY + c] * SCALE + gback[K, s, c].astype(jnp.float32)).astype(jnp.bfloat16)
            o_start(s, K, k)
            g_copy(s, V, k).wait_recv()
            osend[V, s, c] = (dv[s, NY + c] + gback[V, s, c].astype(jnp.float32)).astype(jnp.bfloat16)
            o_start(s, V, k)

    x_start(0, K)
    x_start(0, V)
    x_start(0, Q)
    for to in range(NY):
        for s in range(HPD):
            part_of = marks_in[:, s * half + to * HD:s * half + (to + 1) * HD].astype(jnp.float32)
            marks_own[to, :, s * HD:(s + 1) * HD] = jnp.concatenate([part_of, jnp.zeros((8 - CB, HD), jnp.float32)])
    row = lax.broadcasted_iota(jnp.int32, (CB, CH), 0)
    col = lax.broadcasted_iota(jnp.int32, (CB, CH), 1)
    of_block = (col // BLOCK == row).astype(jnp.bfloat16)
    sel_own[...] = dot(sel_in[...].astype(jnp.float32).astype(jnp.bfloat16), of_block, TN)
    mark_loc.start()
    sel_loc.start()
    for k in range(1, NY):
        mark_copy(k).start()
        sel_copy(k).start()

    ot[...] = jnp.zeros_like(ot)
    dqt[...] = jnp.zeros_like(dqt)
    dk[...] = jnp.zeros_like(dk)
    dv[...] = jnp.zeros_like(dv)
    dgates[...] = jnp.zeros_like(dgates)
    dm[...] = jnp.zeros_like(dm)

    x_wait(0, K)
    y_start(0, K)
    z_copy(0, K, 0).start()
    x_start(0, D)
    x_wait(0, V)
    y_start(0, V)
    z_copy(0, V, 0).start()
    x_start(1, K)
    mark_loc.wait()
    sel_loc.wait()
    for k in range(1, NY):
        mark_arrival(k).wait_recv()
        sel_arrival(k).wait_recv()
    mark_up.start()
    z_pass(0, K)
    x_wait(0, Q)
    y_start(0, Q)
    x_start(1, V)
    z_pass(0, V)
    x_wait(0, D)
    y_start(0, D)
    x_start(1, Q)
    x_wait(1, K)
    y_start(1, K)
    z_copy(1, K, 0).start()
    x_start(1, D)
    y_wait(0, Q)
    mark_up.wait_recv()
    prepare(0)
    x_wait(1, V)
    y_start(1, V)
    z_copy(1, V, 0).start()
    y_wait(0, D)
    chunk(0, 0)
    z_pass(1, K)
    chunk(0, 1)
    z_pass(1, V)
    chunk(0, 2)
    x_wait(1, Q)
    y_start(1, Q)
    chunk(0, 3)
    x_wait(1, D)
    y_start(1, D)
    close(0)
    y_wait(1, Q)
    prepare(1)
    finish(0, (0, 1))
    y_wait(1, D)
    chunk(1, 0)
    finish(0, (2,))
    chunk(1, 1)
    finish(0, (3,))
    chunk(1, 2)
    chunk(1, 3)
    close(1)

    dmsend[...] = dm[0:NY]
    dm_back = remote(dmsend, dmback, gm_send, gm_recv, z=down)
    dm_back.start()
    finish(1, range(NY))
    dm_back.wait_recv()
    dm[NY:] = dm[NY:] + dmback[...]

    def dm_copy(k):
        to = from_y(k)
        return remote(dm.at[NY + to], dm_out.at[:, cols(y, feat)], s_send.at[2, k], s_recv.at[2, k], y=to)

    def dm_arrival(k):
        return remote(dm.at[NY], dm_out.at[:, cols(to_y(k), feat)], s_send.at[2, k], s_recv.at[2, k], y=to_y(k))

    dm_local = pltpu.make_async_copy(dm.at[NY + y], dm_out.at[:, cols(y, feat)], s_loc.at[2])
    for k in range(1, NY):
        dm_copy(k).start()
    dm_local.start()

    for s in range(HPD):
        for a in range(4):
            for c in x_copies(s, a):
                c.wait_send()
            for k in range(1, NY):
                y_copy(s, a, k).wait_send()
                o_copy(s, a, k).wait_send()
                o_arrival(s, a, k).wait_recv()
            o_local(s, a).wait()
        for a in (K, V):
            for k in range(NY):
                z_copy(s, a, k).wait_send()
                g_copy(s, a, k).wait_send()
    for k in range(1, NY):
        mark_copy(k).wait_send()
        sel_copy(k).wait_send()
        dm_copy(k).wait_send()
        dm_arrival(k).wait_recv()
    dm_local.wait()
    mark_up.wait_send()
    dm_back.wait_send()


def hand_over(*refs):
    for n in range(4):
        refs[5 + n][...] = refs[n][...]
    for y in range(NY):
        for s in range(HPD):
            to = (s * NY + y) * HD
            at = (y * HPD + s) * HD
            refs[9][:, to:to + HD] = refs[4][0:CB, at:at + HD].astype(jnp.bfloat16)


def per_device(queries, keys, values, landmarks, grad_out, selections):
    nz, nh = lax.axis_size("z"), lax.axis_size("head")
    width = landmarks.shape[1]
    b, f = jnp.bfloat16, jnp.float32
    hbm, vmem = pl.BlockSpec(memory_space=pl.ANY), pl.BlockSpec(memory_space=pltpu.VMEM)
    big = jax.ShapeDtypeStruct((CH, width), b)
    tall = NY * CH
    feat = HPD * HD
    sem = pltpu.SemaphoreType.DMA
    dk, dv, o, dq, dm = pl.pallas_call(
        lambda *refs: kernel(nz, nh, *refs),
        out_shape=[big] * 4 + [jax.ShapeDtypeStruct((8, width), f)],
        in_specs=[hbm] * 4 + [vmem] * 2,
        out_specs=[hbm] * 4 + [hbm],
        scratch_shapes=[
            pltpu.VMEM((HPD, 4, CH, NY * HD), b),
            pltpu.VMEM((HPD, 2 * tall, HD), b),
            pltpu.VMEM((HPD, 2 * tall, HD), b),
            pltpu.VMEM((HPD, tall, HD), b),
            pltpu.VMEM((HPD, tall, HD), b),
            pltpu.VMEM((NY, 8, feat), f),
            pltpu.VMEM((selections.shape[1], CH), f),
            pltpu.VMEM((8, 8, feat), f),
            pltpu.VMEM((NY, selections.shape[1], CH), f),
            pltpu.VMEM((2, HPD, NY, CH, HD), b),
            pltpu.VMEM((2, HPD, NY, CH, HD), b),
            pltpu.VMEM((4, HPD, NY, CH, HD), b),
            pltpu.VMEM((8, 8, feat), f),
            pltpu.VMEM((NY, 8, feat), f),
            pltpu.VMEM((NY, 8, feat), f),
            pltpu.VMEM((HPD, 8, HD, CH), b),
            pltpu.VMEM((HPD, 8, HD, CH), b),
            pltpu.VMEM((HPD, NY, 8, 8, CH), f),
            pltpu.VMEM((HPD, NY, 8, 8, CH), f),
            pltpu.VMEM((HPD, NY, HD, CH), f),
            pltpu.VMEM((HPD, NY, HD, CH), f),
            pltpu.VMEM((HPD, 8, CH, HD), f),
            pltpu.VMEM((HPD, 8, CH, HD), f),
            sem((8,)), sem((8, 8)), sem((8, 8)),
            sem((8,)), sem((8, 4)), sem((8, 4)),
            sem((4, 4)), sem((4, 4)),
            sem((3,)), sem((3, 4)), sem((3, 4)),
            sem, sem,
            sem((4, 4)), sem((4, 4)), sem, sem,
            sem((8,)), sem((8, 4)), sem((8, 4)),
        ],
        compiler_params=pltpu.CompilerParams(
            collective_id=0, has_side_effects=True, vmem_limit_bytes=63 * 1024 * 1024),
    )(keys, values, queries, grad_out, landmarks, selections)
    piece = pl.BlockSpec((CH // 4, width), lambda n: (n, 0))
    return pl.pallas_call(
        hand_over,
        grid=(4,),
        out_shape=[big] * 4 + [jax.ShapeDtypeStruct((CB, width), b)],
        in_specs=[piece] * 4 + [pl.BlockSpec((8, width), lambda n: (0, 0))],
        out_specs=[piece] * 4 + [pl.BlockSpec((CB, width), lambda n: (0, 0))],
        compiler_params=pltpu.CompilerParams(vmem_limit_bytes=60 * 1024 * 1024),
    )(o, dq, dk, dv, dm)


def solution(mesh):
    shape = (mesh.shape["seq"] // NY, NY, mesh.shape["head"])
    split = jax.sharding.Mesh(mesh.devices.reshape(shape), ("z", "y", "head"))
    rows_all = P(("z", "y", "head"), None)
    out = P(("z", "y"), "head")
    return jax.shard_map(
        per_device, mesh=split,
        in_specs=(rows_all, rows_all, rows_all, out, rows_all, P(("z", "y"), None)),
        out_specs=(out,) * 5, check_vma=False)
```

```python
import jax
import jax.numpy as jnp
from jax import lax
from jax.experimental import pallas as pl
from jax.experimental.pallas import tpu as pltpu
from jax.sharding import PartitionSpec as P

HD = 128
BLOCK = 64
HPD = 2
CH = 256
CB = CH // BLOCK
NY = 4
SCALE = HD ** (-0.5)
LOG2E = 1.4426950408889634
NT = (((1,), (1,)), ((), ()))
NN = (((1,), (0,)), ((), ()))
TN = (((0,), (0,)), ((), ()))
MESH = pl.DeviceIdType.MESH
K, V, Q, D = 0, 1, 2, 3


def dot(a, b, dims):
    return lax.dot_general(a, b, dims, preferred_element_type=jnp.float32)


def rows(c):
    return pl.ds(pl.multiple_of(c * CH, CH), CH)


def gate_tile(s, t, first, q, marks, sel, gates):
    row = lax.broadcasted_iota(jnp.int32, (64, CH), 0)
    sub = row % 8
    block = first + (row // 8) * CB + sub
    block = jnp.where((sub < CB) & (block >= 0), block, -2).astype(jnp.float32)
    picks = sel[t]
    live = block == picks[0:1]
    for e in range(1, picks.shape[0]):
        live = live | (block == picks[e:e + 1])
    mk = marks[:, :, s * HD:(s + 1) * HD].reshape(64, HD).astype(jnp.bfloat16)
    coarse = dot(mk, q[s, rows(t), :], NT) * SCALE
    coarse = jnp.where(live, coarse, -1e30)
    top = jnp.max(coarse, axis=0, keepdims=True)
    ex = jnp.exp(coarse - top)
    gates[s, t] = (ex / jnp.sum(ex, axis=0, keepdims=True)).reshape(8, 8, CH)


def chunk_cells(h, c, q, d, k, v, kt, vt, gates, dgates, ot, dqt, dk, dv):
    cells = [(t, jnp.where(t <= c, c, c + NY), False) for t in range(NY)] + [(c, c + NY, True)]

    def first(i):
        t, kc, _ = cells[i]
        return (dot(k[h, rows(kc), :], q[h, rows(t), :], NT), dot(v[h, rows(kc), :], d[h, rows(t), :], NT))

    def middle(i, s, g):
        t, kc, diag = cells[i]
        if diag:
            row = lax.broadcasted_iota(jnp.int32, (CH, CH), 0)
            col = lax.broadcasted_iota(jnp.int32, (CH, CH), 1)
            s = jnp.where(row > col, -1e30, s)
        s = s.reshape(CB, BLOCK, CH)
        g = g.reshape(CB, BLOCK, CH)
        top = jnp.max(s, axis=1, keepdims=True)
        p = jnp.exp2((s - top) * (SCALE * LOG2E))
        rz = 1.0 / jnp.sum(p, axis=1, keepdims=True)
        dg = jnp.sum(p * g, axis=1, keepdims=True) * rz
        gate = gates[h, t, kc][0:CB].reshape(CB, 1, CH)
        w = p * (gate * rz)
        ds = w * (g - dg)
        dgates[h, t, kc, 0:CB] = dg.reshape(CB, CH)
        return w.astype(jnp.bfloat16).reshape(CH, CH), ds.astype(jnp.bfloat16).reshape(CH, CH)

    def last(i, wb, sb):
        t, kc, _ = cells[i]
        ot[h, t] += dot(vt[h, kc], wb, NN)
        dqt[h, t] += dot(kt[h, kc], sb, NN)
        dv[h, kc] += dot(wb, d[h, rows(t), :], NN)
        dk[h, kc] += dot(sb, q[h, rows(t), :], NN)

    ready, done = first(0), None
    for i in range(len(cells)):
        following = first(i + 1) if i + 1 < len(cells) else None
        pair = middle(i, *ready)
        if done is not None:
            last(i - 1, *done)
        ready, done = following, pair
    last(len(cells) - 1, *done)


def close_tile(s, t, q, marks, gates, dgates, ot, dqt, dm, osend):
    gate = gates[s, t].reshape(64, CH)
    dg = dgates[s, t].reshape(64, CH)
    dc = gate * (dg - jnp.sum(gate * dg, axis=0, keepdims=True))
    dcb = dc.astype(jnp.bfloat16)
    mk = marks[:, :, s * HD:(s + 1) * HD].reshape(64, HD).astype(jnp.bfloat16)
    dq = dqt[s, t] + dot(mk, dcb, TN)
    osend[Q, s, t] = ot[s, t].T.astype(jnp.bfloat16)
    osend[D, s, t] = (dq * SCALE).T.astype(jnp.bfloat16)
    dm[:, :, s * HD:(s + 1) * HD] += (dot(dcb, q[s, rows(t), :], NN) * SCALE).reshape(8, 8, HD)


def remote(src, dst, send, recv, **where):
    return pltpu.make_async_remote_copy(
        src_ref=src, dst_ref=dst, send_sem=send, recv_sem=recv, device_id=where, device_id_type=MESH)


def kernel(nz, nh, k_in, v_in, q_in, d_in, marks_in, sel_in,
           dk_out, dv_out, o_out, dq_out, dm_out,
           xb, k_win, v_win, q_all, d_all, marks_own, sel_own, marks, sel, gsend, gback, osend, dm, dmback, dmsend,
           kt, vt, gates, dgates, ot, dqt, dk, dv,
           x_loc, x_send, x_recv, y_loc, y_send, y_recv, z_send, z_recv,
           s_loc, s_send, s_recv, mz_send, mz_recv, g_send, g_recv, gm_send, gm_recv,
           o_loc, o_send, o_recv):
    z, y, h = lax.axis_index("z"), lax.axis_index("y"), lax.axis_index("head")
    up, down = lax.rem(z + 1, nz), lax.rem(z + nz - 1, nz)
    inputs = (k_in, v_in, q_in, d_in)
    outs = (dk_out, dv_out, o_out, dq_out)
    part = k_in.shape[0]
    half = NY * HD
    wide = HPD * half
    mine = pl.ds(pl.multiple_of(h * part, part), part)

    def to_y(k):
        return lax.rem(y + k, NY)

    def from_y(k):
        return lax.rem(y + NY - k, NY)

    def cols(c, n=HD, base=0):
        return pl.ds(pl.multiple_of(base + c * n, HD), n)

    barrier = pltpu.get_barrier_semaphore()
    for k in range(1, nh):
        pl.semaphore_signal(barrier, inc=1, device_id={"head": lax.rem(h + k, nh)}, device_id_type=MESH)
    for k in range(1, NY):
        pl.semaphore_signal(barrier, inc=1, device_id={"y": to_y(k)}, device_id_type=MESH)
    for other in (up, down):
        pl.semaphore_signal(barrier, inc=1, device_id={"z": other}, device_id_type=MESH)
    pl.semaphore_wait(barrier, nh + NY)

    def x_copies(s, a):
        out = []
        for k in range(1, nh):
            to = lax.rem(h + k, nh)
            out.append(remote(
                inputs[a].at[:, pl.ds(pl.multiple_of(to * wide + s * half, half), half)],
                xb.at[s, a, mine, :], x_send.at[4 * s + a, k], x_recv.at[4 * s + a, k], head=to))
        return out

    def x_local(s, a):
        return pltpu.make_async_copy(
            inputs[a].at[:, pl.ds(pl.multiple_of(h * wide + s * half, half), half)],
            xb.at[s, a, mine, :], x_loc.at[4 * s + a])

    def x_start(s, a):
        for c in x_copies(s, a):
            c.start()
        x_local(s, a).start()

    def x_wait(s, a):
        for c in x_copies(s, a):
            c.wait_recv()
        x_local(s, a).wait()

    def own_rows(s, a, c):
        if a == K:
            return k_win.at[s, rows(NY + c), :]
        if a == V:
            return v_win.at[s, rows(NY + c), :]
        return (q_all if a == Q else d_all).at[s, rows(c), :]

    def y_copy(s, a, k):
        to = to_y(k)
        return remote(xb.at[s, a, :, cols(to)], own_rows(s, a, y),
                      y_send.at[4 * s + a, k], y_recv.at[4 * s + a, k], y=to)

    def y_arrival(s, a, k):
        return remote(xb.at[s, a, :, cols(y)], own_rows(s, a, from_y(k)),
                      y_send.at[4 * s + a, k], y_recv.at[4 * s + a, k], y=to_y(k))

    def y_local(s, a):
        return pltpu.make_async_copy(xb.at[s, a, :, cols(y)], own_rows(s, a, y), y_loc.at[4 * s + a])

    def y_start(s, a):
        for k in range(1, NY):
            y_copy(s, a, k).start()
        y_local(s, a).start()

    def y_wait(s, a):
        for k in range(1, NY):
            y_arrival(s, a, k).wait_recv()
        y_local(s, a).wait()

    def z_copy(s, a, k):
        win = (k_win, v_win)[a]
        c = from_y(k)
        src = xb.at[s, a, :, cols(y)] if k == 0 else win.at[s, rows(NY + c), :]
        return remote(src, win.at[s, rows(c), :], z_send.at[2 * s + a, k], z_recv.at[2 * s + a, k], z=up)

    def z_pass(s, a):
        for k in range(1, NY):
            y_arrival(s, a, k).wait_recv()
            z_copy(s, a, k).start()
        y_local(s, a).wait()

    feat = HPD * HD
    mark_loc = pltpu.make_async_copy(marks_own.at[y], marks.at[NY + y], s_loc.at[0])
    sel_loc = pltpu.make_async_copy(sel_own, sel.at[y], s_loc.at[1])

    def mark_copy(k):
        to = to_y(k)
        return remote(marks_own.at[to], marks.at[NY + y], s_send.at[0, k], s_recv.at[0, k], y=to)

    def mark_arrival(k):
        return remote(marks_own.at[y], marks.at[NY + from_y(k)],
                      s_send.at[0, k], s_recv.at[0, k], y=to_y(k))

    def sel_copy(k):
        return remote(sel_own, sel.at[y], s_send.at[1, k], s_recv.at[1, k], y=to_y(k))

    def sel_arrival(k):
        return remote(sel_own, sel.at[from_y(k)], s_send.at[1, k], s_recv.at[1, k], y=to_y(k))

    mark_up = remote(marks.at[pl.ds(NY, NY)], marks.at[pl.ds(0, NY)], mz_send, mz_recv, z=up)

    args = (q_all, d_all, k_win, v_win, kt, vt, gates, dgates, ot, dqt, dk, dv)
    first = (z - 1) * (NY * CB)

    def transpose_chunk(s, kc):
        kt[s, kc] = k_win[s, rows(kc), :].T
        vt[s, kc] = v_win[s, rows(kc), :].T

    def g_copy(s, a, k):
        c = from_y(k)
        return remote(gsend.at[a, s, c], gback.at[a, s, c], g_send.at[2 * s + a, k], g_recv.at[2 * s + a, k], z=down)

    def prepare(s):
        @pl.loop(0, NY)
        def _(t):
            gate_tile(s, t, first, q_all, marks, sel, gates)

    def chunk(s, k):
        c = from_y(k)
        z_copy(s, K, k).wait_recv()
        z_copy(s, V, k).wait_recv()
        transpose_chunk(s, c)
        transpose_chunk(s, c + NY)
        chunk_cells(s, c, *args)
        gsend[K, s, c] = (dk[s, c] * SCALE).astype(jnp.bfloat16)
        g_copy(s, K, k).start()
        gsend[V, s, c] = dv[s, c].astype(jnp.bfloat16)
        g_copy(s, V, k).start()

    def o_copy(s, a, k):
        to = from_y(k)
        return remote(osend.at[a, s, to], outs[a].at[:, cols(y, HD, s * half)],
                      o_send.at[4 * s + a, k], o_recv.at[4 * s + a, k], y=to)

    def o_arrival(s, a, k):
        return remote(osend.at[a, s, 0], outs[a].at[:, cols(to_y(k), HD, s * half)],
                      o_send.at[4 * s + a, k], o_recv.at[4 * s + a, k], y=to_y(k))

    def o_local(s, a):
        return pltpu.make_async_copy(osend.at[a, s, y], outs[a].at[:, cols(y, HD, s * half)], o_loc.at[4 * s + a])

    def o_start(s, a, k):
        if k == 0:
            o_local(s, a).start()
        else:
            o_copy(s, a, k).start()

    def close(s):
        for k in (1, 2, 3, 0):
            close_tile(s, from_y(k), q_all, marks, gates, dgates, ot, dqt, dm, osend)
            o_start(s, Q, k)
            o_start(s, D, k)

    def finish(s, turns):
        for k in turns:
            c = from_y(k)
            g_copy(s, K, k).wait_recv()
            osend[K, s, c] = (dk[s, NY + c] * SCALE + gback[K, s, c].astype(jnp.float32)).astype(jnp.bfloat16)
            o_start(s, K, k)
            g_copy(s, V, k).wait_recv()
            osend[V, s, c] = (dv[s, NY + c] + gback[V, s, c].astype(jnp.float32)).astype(jnp.bfloat16)
            o_start(s, V, k)

    x_start(0, K)
    x_start(0, V)
    x_start(0, Q)
    for to in range(NY):
        for s in range(HPD):
            part_of = marks_in[:, s * half + to * HD:s * half + (to + 1) * HD].astype(jnp.float32)
            marks_own[to, :, s * HD:(s + 1) * HD] = jnp.concatenate([part_of, jnp.zeros((8 - CB, HD), jnp.float32)])
    row = lax.broadcasted_iota(jnp.int32, (CB, CH), 0)
    col = lax.broadcasted_iota(jnp.int32, (CB, CH), 1)
    of_block = (col // BLOCK == row).astype(jnp.bfloat16)
    sel_own[...] = dot(sel_in[...].astype(jnp.float32).astype(jnp.bfloat16), of_block, TN)
    mark_loc.start()
    sel_loc.start()
    for k in range(1, NY):
        mark_copy(k).start()
        sel_copy(k).start()

    ot[...] = jnp.zeros_like(ot)
    dqt[...] = jnp.zeros_like(dqt)
    dk[...] = jnp.zeros_like(dk)
    dv[...] = jnp.zeros_like(dv)
    dgates[...] = jnp.zeros_like(dgates)
    dm[...] = jnp.zeros_like(dm)

    x_wait(0, K)
    y_start(0, K)
    z_copy(0, K, 0).start()
    x_start(0, D)
    x_wait(0, V)
    y_start(0, V)
    z_copy(0, V, 0).start()
    x_start(1, K)
    mark_loc.wait()
    sel_loc.wait()
    for k in range(1, NY):
        mark_arrival(k).wait_recv()
        sel_arrival(k).wait_recv()
    mark_up.start()
    z_pass(0, K)
    x_wait(0, Q)
    y_start(0, Q)
    x_start(1, V)
    z_pass(0, V)
    x_wait(0, D)
    y_start(0, D)
    x_start(1, Q)
    x_wait(1, K)
    y_start(1, K)
    z_copy(1, K, 0).start()
    x_start(1, D)
    y_wait(0, Q)
    mark_up.wait_recv()
    prepare(0)
    x_wait(1, V)
    y_start(1, V)
    z_copy(1, V, 0).start()
    y_wait(0, D)
    chunk(0, 0)
    z_pass(1, K)
    chunk(0, 1)
    z_pass(1, V)
    chunk(0, 2)
    x_wait(1, Q)
    y_start(1, Q)
    chunk(0, 3)
    x_wait(1, D)
    y_start(1, D)
    close(0)
    y_wait(1, Q)
    prepare(1)
    finish(0, (0, 1))
    y_wait(1, D)
    chunk(1, 0)
    finish(0, (2,))
    chunk(1, 1)
    finish(0, (3,))
    chunk(1, 2)
    chunk(1, 3)
    close(1)

    dmsend[...] = dm[0:NY]
    dm_back = remote(dmsend, dmback, gm_send, gm_recv, z=down)
    dm_back.start()
    finish(1, (0, 1))
    dm_back.wait_recv()
    dm[NY:] = dm[NY:] + dmback[...]

    def dm_copy(k):
        to = from_y(k)
        return remote(dm.at[NY + to], dm_out.at[:, cols(y, feat)], s_send.at[2, k], s_recv.at[2, k], y=to)

    def dm_arrival(k):
        return remote(dm.at[NY], dm_out.at[:, cols(to_y(k), feat)], s_send.at[2, k], s_recv.at[2, k], y=to_y(k))

    dm_local = pltpu.make_async_copy(dm.at[NY + y], dm_out.at[:, cols(y, feat)], s_loc.at[2])
    for k in range(1, NY):
        dm_copy(k).start()
    dm_local.start()
    finish(1, (2, 3))

    for s in range(HPD):
        for a in range(4):
            for c in x_copies(s, a):
                c.wait_send()
            for k in range(1, NY):
                y_copy(s, a, k).wait_send()
                o_copy(s, a, k).wait_send()
                o_arrival(s, a, k).wait_recv()
            o_local(s, a).wait()
        for a in (K, V):
            for k in range(NY):
                z_copy(s, a, k).wait_send()
                g_copy(s, a, k).wait_send()
    for k in range(1, NY):
        mark_copy(k).wait_send()
        sel_copy(k).wait_send()
        dm_copy(k).wait_send()
        dm_arrival(k).wait_recv()
    dm_local.wait()
    mark_up.wait_send()
    dm_back.wait_send()


def hand_over(*refs):
    for n in range(4):
        refs[5 + n][...] = refs[n][...]
    for y in range(NY):
        for s in range(HPD):
            to = (s * NY + y) * HD
            at = (y * HPD + s) * HD
            refs[9][:, to:to + HD] = refs[4][0:CB, at:at + HD].astype(jnp.bfloat16)


def per_device(queries, keys, values, landmarks, grad_out, selections):
    nz, nh = lax.axis_size("z"), lax.axis_size("head")
    width = landmarks.shape[1]
    b, f = jnp.bfloat16, jnp.float32
    hbm, vmem = pl.BlockSpec(memory_space=pl.ANY), pl.BlockSpec(memory_space=pltpu.VMEM)
    big = jax.ShapeDtypeStruct((CH, width), b)
    tall = NY * CH
    feat = HPD * HD
    sem = pltpu.SemaphoreType.DMA
    dk, dv, o, dq, dm = pl.pallas_call(
        lambda *refs: kernel(nz, nh, *refs),
        out_shape=[big] * 4 + [jax.ShapeDtypeStruct((8, width), f)],
        in_specs=[hbm] * 4 + [vmem] * 2,
        out_specs=[hbm] * 4 + [hbm],
        scratch_shapes=[
            pltpu.VMEM((HPD, 4, CH, NY * HD), b),
            pltpu.VMEM((HPD, 2 * tall, HD), b),
            pltpu.VMEM((HPD, 2 * tall, HD), b),
            pltpu.VMEM((HPD, tall, HD), b),
            pltpu.VMEM((HPD, tall, HD), b),
            pltpu.VMEM((NY, 8, feat), f),
            pltpu.VMEM((selections.shape[1], CH), f),
            pltpu.VMEM((8, 8, feat), f),
            pltpu.VMEM((NY, selections.shape[1], CH), f),
            pltpu.VMEM((2, HPD, NY, CH, HD), b),
            pltpu.VMEM((2, HPD, NY, CH, HD), b),
            pltpu.VMEM((4, HPD, NY, CH, HD), b),
            pltpu.VMEM((8, 8, feat), f),
            pltpu.VMEM((NY, 8, feat), f),
            pltpu.VMEM((NY, 8, feat), f),
            pltpu.VMEM((HPD, 8, HD, CH), b),
            pltpu.VMEM((HPD, 8, HD, CH), b),
            pltpu.VMEM((HPD, NY, 8, 8, CH), f),
            pltpu.VMEM((HPD, NY, 8, 8, CH), f),
            pltpu.VMEM((HPD, NY, HD, CH), f),
            pltpu.VMEM((HPD, NY, HD, CH), f),
            pltpu.VMEM((HPD, 8, CH, HD), f),
            pltpu.VMEM((HPD, 8, CH, HD), f),
            sem((8,)), sem((8, 8)), sem((8, 8)),
            sem((8,)), sem((8, 4)), sem((8, 4)),
            sem((4, 4)), sem((4, 4)),
            sem((3,)), sem((3, 4)), sem((3, 4)),
            sem, sem,
            sem((4, 4)), sem((4, 4)), sem, sem,
            sem((8,)), sem((8, 4)), sem((8, 4)),
        ],
        compiler_params=pltpu.CompilerParams(
            collective_id=0, has_side_effects=True, vmem_limit_bytes=63 * 1024 * 1024),
    )(keys, values, queries, grad_out, landmarks, selections)
    piece = pl.BlockSpec((CH // 4, width), lambda n: (n, 0))
    return pl.pallas_call(
        hand_over,
        grid=(4,),
        out_shape=[big] * 4 + [jax.ShapeDtypeStruct((CB, width), b)],
        in_specs=[piece] * 4 + [pl.BlockSpec((8, width), lambda n: (0, 0))],
        out_specs=[piece] * 4 + [pl.BlockSpec((CB, width), lambda n: (0, 0))],
        compiler_params=pltpu.CompilerParams(vmem_limit_bytes=60 * 1024 * 1024),
    )(o, dq, dk, dv, dm)


def solution(mesh):
    shape = (mesh.shape["seq"] // NY, NY, mesh.shape["head"])
    split = jax.sharding.Mesh(mesh.devices.reshape(shape), ("z", "y", "head"))
    rows_all = P(("z", "y", "head"), None)
    out = P(("z", "y"), "head")
    return jax.shard_map(
        per_device, mesh=split,
        in_specs=(rows_all, rows_all, rows_all, out, rows_all, P(("z", "y"), None)),
        out_specs=(out,) * 5, check_vma=False)
```
